256 devices in a mesh: frame: 128 (over z, y, x_lo, core), head: 2 (over x_hi).
Axes of the slice: x: 4 (x_hi: 2, x_lo: 2; x = x_hi * 2 + x_lo), y: 4, z: 8, core: 2. Of those that a mesh axis runs over, the one named last changes fastest.
Arguments:
- queries: bfloat16 [16384, 1536], P('frame', 'head'), may hold values from -6 to 6
- keys: bfloat16 [16384, 1536], P('frame', 'head'), may hold values from -6 to 6
- values: bfloat16 [16384, 1536], P('frame', 'head'), may hold values from -6 to 6
- w_out: bfloat16 [1536, 1536], P('head'), may hold values from -0.15625 to 0.15625
- grad_proj: bfloat16 [16384, 1536], P('frame', 'head'), may hold values from -24 to 24
- frame_levels: int32 [256], replicated, may hold values from 0 to 2, as said below
Outputs:
- proj: bfloat16 [16384, 1536], P('frame', 'head')
- d_queries: bfloat16 [16384, 1536], P('frame', 'head')
- d_keys: bfloat16 [16384, 1536], P('frame', 'head')
- d_values: bfloat16 [16384, 1536], P('frame', 'head')
- d_wout: bfloat16 [1536, 1536], P('head', 'frame')
The draws below stay inside these ranges and needn't reach their ends.
Inputs may be any that keep to these rules, and one draw needn't show every extreme that they name: `frame_levels`: within each clip the levels never rise along its frames; the counts of frames at levels 0, 1 and 2 in a clip are one of 7 0 9, 7 2 7, 6 3 7, 6 4 6, 6 5 5, 6 7 3, 5 8 3, 5 9 2, 5 10 1.
All inputs are finite; a program needn't handle non-finite values.
Results may differ from the reference program's by a relative error of at most 0.012.
The reference program's roundings to bfloat16 on the way (of `grad_attn`, `weights_low`, `attn` and `dscore`) count: a program that leaves them out, or rounds other values in their place, can miss the bound.
Values may be sent and summed in bfloat16 or wider, within the bound.
A program may use at most 64 MiB of HBM per device.

```python
from functools import partial
import jax
import jax.numpy as jnp
from jax import lax

HEADS = 24
HEAD_DIM = 64
TOK_DEV = 128
CLIP_BLOCKS = 8
FRAMES_CLIP = 16
WIDTH = 1536
TOKENS = 16384
FRAMES = 256
N_FRAME = 128


def drawn_rows(key):
    base = jnp.clip(jax.random.normal(jax.random.fold_in(key, 1), (TOKENS, WIDTH), jnp.float32), -6.0, 6.0)
    return base


def draw_queries(key, part):
    key = jax.random.fold_in(key, 11)
    rows = drawn_rows(key)
    return rows.astype(jnp.bfloat16)


def draw_keys(key, part):
    key = jax.random.fold_in(key, 13)
    rows = drawn_rows(key)
    return rows.astype(jnp.bfloat16)


def draw_frame_levels(key, part):
    key = jax.random.fold_in(key, 7)
    first, second, third = jax.random.split(key, 3)
    clips = FRAMES // FRAMES_CLIP
    full_table = jnp.array([7, 7, 6, 6, 6, 6, 5, 5, 5], jnp.int32)
    half_table = jnp.array([0, 2, 3, 4, 5, 7, 8, 9, 10], jnp.int32)
    pick = jax.random.randint(first, (clips,), 0, 9)
    chosen_clip = jax.random.randint(second, (), 0, clips)
    extreme = jax.random.randint(third, (), 0, 2) * 8
    index = jnp.arange(clips)
    pick = jnp.where(index == chosen_clip, extreme, pick)
    onehot = pick[:, None] == jnp.arange(9)[None, :]
    full_count = jnp.sum(jnp.where(onehot, full_table[None, :], 0), axis=1)
    half_count = jnp.sum(jnp.where(onehot, half_table[None, :], 0), axis=1)
    position = jnp.arange(FRAMES_CLIP)[None, :]
    full_from = FRAMES_CLIP - full_count[:, None]
    half_from = full_from - half_count[:, None]
    levels = jnp.where(position >= full_from, 0, jnp.where(position >= half_from, 1, 2))
    return levels.reshape(FRAMES).astype(jnp.int32)


def raised(drawn, rng, source, target, shards_of, factor):
    owner, partner = [(jnp.arange(drawn.shape[dim]) // (drawn.shape[dim] // shards_of)).reshape([-1 if axis == dim else 1 for axis in range(drawn.ndim)]) for dim in (source, target)]
    chosen = jax.random.permutation(rng, shards_of)[partner]
    strong = (owner == chosen) | (owner == (partner + shards_of // 2) % shards_of)
    return jnp.where(strong, factor * drawn, drawn)


def shard_levels(own_key, extent, cuts, low, high):
    level = 1.0
    for dim, shards_of in cuts:
        steps = jax.random.uniform(jax.random.fold_in(jax.random.fold_in(own_key, 6), dim), (shards_of,), jnp.float32, low / len(cuts), high / len(cuts))
        level = level * jnp.repeat(jnp.exp(steps), extent[dim] // shards_of).reshape((-1,) + (1,) * (len(extent) - 1 - dim))
    return level


def gaussian(rng, dims, width, reach, cuts=(), kind=jnp.bfloat16):
    values = jax.random.normal(rng, dims, jnp.float32) * width
    if len(cuts) > 0:
        values = shard_levels(rng, dims, cuts, -0.22, 0.18) * values
    return jnp.clip(values, min=-reach, max=reach).astype(kind)


def heavy_noise(rng, dims, deviation, most, shards, heavy, kind=jnp.bfloat16):
    entries = deviation * jax.random.normal(rng, dims, jnp.float32)
    if shards:
        entries = entries * shard_levels(rng, dims, shards, -0.22, 0.18)
    return jnp.clip(raised(entries, jax.random.fold_in(rng, 3), *heavy), -most, most).astype(kind)


def setup_inputs(seed: int = 0) -> dict:
    key_list = jax.random.split(jax.random.key(seed), 7)
    return {
        "queries": draw_queries(jax.random.fold_in(key_list[6], 71), 0),
        "keys": draw_keys(jax.random.fold_in(key_list[6], 71), 0),
        "values": gaussian(key_list[2], (TOKENS, WIDTH), 1.0, 6.0, ((0, 128), (1, 2))),
        "w_out": gaussian(key_list[3], (WIDTH, WIDTH), WIDTH ** -0.5, 0.15625, ((0, 2),)),
        "grad_proj": heavy_noise(key_list[4], (TOKENS, WIDTH), 1.0, 24.0, ((0, 128), (1, 2)), (0, 1, 128, 5.5)),
        "frame_levels": draw_frame_levels(jax.random.fold_in(key_list[6], 71), 0),
    }


def contract(left, right, dims_left, dims_right):
    return lax.dot_general(left, right, (((dims_left,), (dims_right,)), ((), ())), preferred_element_type=jnp.float32)


def head_math(mask, scale, operands):
    query, key_rows, value_rows, grad_rows = operands
    scores = contract(query, key_rows, 1, 1) * scale
    masked = jnp.where(mask, scores, -1e30)
    peak = jnp.max(masked, axis=1, keepdims=True)
    peak = jnp.where(jnp.any(mask, axis=1, keepdims=True), peak, 0.0)
    expo = jnp.where(mask, jnp.exp(scores - peak), 0.0)
    total = jnp.sum(expo, axis=1, keepdims=True)
    weights = expo / jnp.where(total > 0.0, total, 1.0)
    weights_low = weights.astype(jnp.bfloat16)
    attended = contract(weights_low, value_rows, 1, 0).astype(jnp.bfloat16)
    delta = jnp.sum(grad_rows.astype(jnp.float32) * attended.astype(jnp.float32), axis=1, keepdims=True)
    dprob = contract(grad_rows, value_rows, 1, 1)
    dscore = (weights * (dprob - delta)).astype(jnp.bfloat16)
    dquery = contract(dscore, key_rows, 1, 0) * scale
    dkey = contract(dscore, query, 0, 0) * scale
    dvalue = contract(weights_low, grad_rows, 0, 0)
    return attended, dquery, dkey, dvalue


def split_heads(rows):
    return rows.reshape(rows.shape[0], HEADS, HEAD_DIM).transpose(1, 0, 2)


def join_heads(stacked):
    return stacked.transpose(1, 0, 2).reshape(stacked.shape[1], HEADS * HEAD_DIM)


def frame_layout(frame_levels):
    sizes = jnp.where(frame_levels == 0, TOK_DEV, jnp.where(frame_levels == 1, TOK_DEV // 4, TOK_DEV // 16)).astype(jnp.int32)
    table = sizes.reshape(N_FRAME // CLIP_BLOCKS, FRAMES_CLIP)
    ends = jnp.cumsum(table, axis=1).astype(jnp.int32)
    return ends - table, ends[:, -1]


def reference(queries, keys, values, w_out, grad_proj, frame_levels):
    block_len = TOK_DEV
    span = (CLIP_BLOCKS + 1) * block_len
    front = (CLIP_BLOCKS - 1) * block_len
    clip_slots = CLIP_BLOCKS * block_len
    scale = HEAD_DIM ** -0.5
    starts, totals = frame_layout(frame_levels)
    slots = jnp.arange(TOKENS, dtype=jnp.int32)
    clip_of = (slots // clip_slots).astype(jnp.int32)
    offset = slots - clip_of * clip_slots
    live = offset < totals[clip_of]
    frame_in = jnp.sum((starts[clip_of] <= offset[:, None]).astype(jnp.int32), axis=1).astype(jnp.int32)
    frame_all = (clip_of * FRAMES_CLIP + frame_in).astype(jnp.int32)
    grad_attn = lax.dot_general(grad_proj, w_out, (((1,), (1,)), ((), ())), preferred_element_type=jnp.float32).astype(jnp.bfloat16)
    key_pad = jnp.pad(keys, ((front, block_len), (0, 0)))
    value_pad = jnp.pad(values, ((front, block_len), (0, 0)))
    live_pad = jnp.pad(live, (front, block_len))
    frame_pad = jnp.pad(frame_all, (front, block_len))
    clip_pad = jnp.pad(clip_of, (front, block_len), constant_values=-1)
    zeros = jnp.zeros((TOKENS + front + block_len, WIDTH), jnp.float32)

    def step(carry, block):
        dkey_acc, dvalue_acc = carry
        start = (block * block_len).astype(jnp.int32)
        query = lax.dynamic_slice_in_dim(queries, start, block_len, 0)
        grad_rows = lax.dynamic_slice_in_dim(grad_attn, start, block_len, 0)
        key_rows = lax.dynamic_slice_in_dim(key_pad, start, span, 0)
        value_rows = lax.dynamic_slice_in_dim(value_pad, start, span, 0)
        frame_query = lax.dynamic_slice_in_dim(frame_all, start, block_len, 0)
        frame_key = lax.dynamic_slice_in_dim(frame_pad, start, span, 0)
        clip_query = lax.dynamic_slice_in_dim(clip_of, start, block_len, 0)
        clip_key = lax.dynamic_slice_in_dim(clip_pad, start, span, 0)
        live_query = lax.dynamic_slice_in_dim(live, start, block_len, 0)
        live_key = lax.dynamic_slice_in_dim(live_pad, start, span, 0)
        mask = live_query[:, None] & live_key[None, :] & (clip_key[None, :] == clip_query[:, None]) & (frame_key[None, :] <= frame_query[:, None])
        attended, dquery, dkey, dvalue = lax.map(partial(head_math, mask, scale), (split_heads(query), split_heads(key_rows), split_heads(value_rows), split_heads(grad_rows)))
        old_key = lax.dynamic_slice_in_dim(dkey_acc, start, span, 0)
        old_value = lax.dynamic_slice_in_dim(dvalue_acc, start, span, 0)
        dkey_acc = lax.dynamic_update_slice_in_dim(dkey_acc, old_key + join_heads(dkey), start, 0)
        dvalue_acc = lax.dynamic_update_slice_in_dim(dvalue_acc, old_value + join_heads(dvalue), start, 0)
        return (dkey_acc, dvalue_acc), (join_heads(attended), join_heads(dquery).astype(jnp.bfloat16))

    blocks = jnp.arange(N_FRAME, dtype=jnp.int32)
    (dkey_acc, dvalue_acc), (attn_blocks, dquery_blocks) = lax.scan(step, (zeros, zeros), blocks)
    attn = attn_blocks.reshape(TOKENS, WIDTH)
    proj = jnp.dot(attn, w_out, preferred_element_type=jnp.float32).astype(jnp.bfloat16)
    d_wout = lax.dot_general(attn, grad_proj, (((0,), (0,)), ((), ())), preferred_element_type=jnp.float32).astype(jnp.bfloat16)
    d_queries = dquery_blocks.reshape(TOKENS, WIDTH)
    d_keys = dkey_acc[front:front + TOKENS].astype(jnp.bfloat16)
    d_values = dvalue_acc[front:front + TOKENS].astype(jnp.bfloat16)
    return proj, d_queries, d_keys, d_values, d_wout
```

```python
import functools
import math

import jax
import jax.numpy as jnp
from jax import lax
from jax.experimental import pallas as pl
from jax.experimental.pallas import tpu as pltpu
from jax.sharding import PartitionSpec as P

MESH = pl.DeviceIdType.MESH
BF = jnp.bfloat16
F32 = jnp.float32
HD = 64
BLK = 128
QB = 256
SLOTS = 1024
FEAT = 768
WIDTH = 1536
FRAMES_CLIP = 16
EXP_SCALE = HD ** (-0.5) * math.log2(math.e)


def mm(left, right, dl, dr):
    return lax.dot_general(left, right, (((dl,), (dr,)), ((), ())), preferred_element_type=F32)


def lanes(block):
    return pl.ds(pl.multiple_of(block * BLK, BLK), BLK)


def kernel(
    q_ref, k_ref, v_ref, w_ref, g_ref, lev_ref,
    proj_ref, dq_ref, dk_ref, dv_ref, dw_ref,
    xt, rx, dat, rd, gfull, gt, gy, nat, lim_ref, prob, low, dsb,
    ot, att, attn, pown, psend, precv, acc, xc, dqkv, dkvc, rout,
    ay, dfull, zs, rz, fin, rf,
    s_x, s_xf, r_xa, r_xc, s_d, s_df, r_da, r_dc, s_g, r_g, s_gy, r_gy,
    s_at, s_atc, r_at, s_ay, r_ay, s_p, r_p, s_xc, r_xc2, s_o, s_oq, s_okv, r_o, r_oq,
    s_z, r_z, s_f, r_f,
):
    me = lax.axis_index("frame")
    hd = lax.axis_index("head")
    c = me % 2
    xl = (me // 2) % 2
    y = (me // 4) % 4
    z = me // 16
    s = me % 8
    clip8 = me - s
    j = s // 2
    sib = me + 1 - 2 * c
    pos = y * 2 + c
    others = (3 - j, j + 1 - 2 * (j % 2), (j + 2) % 4)

    def rcopy(src, dst, ss, rs, dev, head=hd):
        return pltpu.make_async_remote_copy(
            src_ref=src, dst_ref=dst, send_sem=ss, recv_sem=rs,
            device_id=(dev, head), device_id_type=MESH,
        )

    def lcopy(src, dst, sem):
        return pltpu.make_async_copy(src, dst, sem)

    def ydev(p):
        return z * 16 + (p // 2) * 4 + xl * 2 + p % 2

    def zdev(zz):
        return zz * 16 + me % 16

    bar = pltpu.get_barrier_semaphore()
    for d in range(1, 8):
        pl.semaphore_signal(bar, inc=1, device_id=(clip8 + (s + d) % 8, hd), device_id_type=MESH)
        pl.semaphore_signal(bar, inc=1, device_id=(zdev((z + d) % 8), hd), device_id_type=MESH)
    pl.semaphore_signal(bar, inc=1, device_id=(me, 1 - hd), device_id_type=MESH)
    yh = (y // 2) * 2
    for n in range(4):
        far = (yh + 2) % 4 + n // 2
        pl.semaphore_signal(
            bar, inc=1, device_id=(z * 16 + far * 4 + xl * 2 + n % 2, hd), device_id_type=MESH
        )

    for i, ref in enumerate((q_ref, k_ref, v_ref)):
        for t in range(6):
            tile = ref[:, t * BLK:(t + 1) * BLK].T
            xt[2 * t, i] = tile[:HD]
            xt[2 * t + 1, i] = tile[HD:]
    pl.semaphore_wait(bar, 19)

    gsend = rcopy(g_ref, gfull.at[:, pl.ds(pl.multiple_of(hd * FEAT, BLK), FEAT)], s_g.at[0], r_g.at[0], me, 1 - hd)
    gsend.start()
    gown = lcopy(g_ref, gfull.at[:, pl.ds(pl.multiple_of(hd * FEAT, BLK), FEAT)], s_g.at[1])
    gown.start()

    def scatter_plan(src, dst, ss, ra, rc):
        remote = []
        for n, jj in enumerate(others):
            base = clip8 + jj * 2
            remote.append(rcopy(src.at[3 * jj], dst.at[0, ..., lanes(s)], ss.at[3 * n], ra.at[s], base))
            remote.append(rcopy(src.at[3 * jj + 1], dst.at[0, ..., lanes(s)], ss.at[3 * n + 1], ra.at[s], base + 1))
            remote.append(rcopy(src.at[3 * jj + 2], dst.at[1, ..., lanes(s)], ss.at[3 * n + 2], rc.at[s], base + c))
        remote.append(rcopy(src.at[3 * j + 1 - c], dst.at[0, ..., lanes(s)], ss.at[9], ra.at[s], sib))
        remote.append(rcopy(src.at[3 * j + 2], dst.at[1, ..., lanes(s)], ss.at[10], rc.at[s], sib))
        local = [
            lcopy(src.at[3 * j + c], dst.at[0, ..., lanes(s)], ra.at[s]),
            lcopy(src.at[3 * j + 2], dst.at[1, ..., lanes(s)], rc.at[s]),
        ]
        return remote, local

    def wait_own(src, dst, ra, rc):
        for b in range(8):
            lcopy(src.at[0], dst.at[0, ..., lanes(b)], ra.at[b]).wait()

    def forward_shared(src, dst, fs, rc):
        plan = []
        for n, jj in enumerate(others):
            b = jj * 2 + c
            lcopy(src.at[0], dst.at[1, ..., lanes(b)], rc.at[b]).wait()
            copy = rcopy(dst.at[1, ..., lanes(b)], dst.at[1, ..., lanes(b)], fs.at[n], rc.at[b], sib)
            copy.start()
            plan.append(copy)
        lcopy(src.at[0], dst.at[1, ..., lanes(s)], rc.at[s]).wait()
        return plan

    def wait_shared(src, dst, rc):
        for jj in range(4):
            b = jj * 2 + 1 - c
            lcopy(src.at[0], dst.at[1, ..., lanes(b)], rc.at[b]).wait()

    x_remote, x_local = scatter_plan(xt, rx, s_x, r_xa, r_xc)
    for copy in x_remote + x_local:
        copy.start()

    slot_iota = lax.broadcasted_iota(jnp.int32, (1, SLOTS), 1)
    seen = jnp.zeros((1, SLOTS), jnp.int32)
    start = jnp.int32(0)
    for f in range(FRAMES_CLIP):
        level = lev_ref[(me // 8) * FRAMES_CLIP + f]
        end = start + jnp.where(level == 0, BLK, jnp.where(level == 1, BLK // 4, BLK // 16))
        seen = jnp.where((slot_iota >= start) & (slot_iota < end), end, seen)
        start = end
    lim_ref[...] = seen

    gown.wait()
    gsend.wait_recv()
    for t in range(3):
        part = mm(w_ref[t * QB:(t + 1) * QB, :], gfull[...], 1, 1).astype(BF)
        for n in range(4):
            dat[4 * t + n] = part[n * HD:(n + 1) * HD]
    d_remote, d_local = scatter_plan(dat, rd, s_d, r_da, r_dc)
    for copy in d_remote + d_local:
        copy.start()

    for t in range(12):
        tile = gfull[:, t * BLK:(t + 1) * BLK].T
        for n in range(8):
            row = t * BLK + n * 16
            gt[row // 192, (row % 192) // 48, row % 48:row % 48 + 16, :] = tile[n * 16:(n + 1) * 16]
    gy_remote = []
    for m in range(1, 8):
        p = (pos + m) % 8
        gy_remote.append(rcopy(gt.at[:, p // 2], gy.at[:, :, lanes(pos)], s_gy.at[m], r_gy.at[pos], ydev(p)))
    gy_local = lcopy(gt.at[:, y], gy.at[:, :, lanes(pos)], r_gy.at[pos])

    x_fwd = forward_shared(xt, rx, s_xf, r_xc)
    for copy in gy_remote:
        copy.start()
    gy_local.start()
    wait_own(xt, rx, r_xa, r_xc)

    def naturals(slot):
        for i in range(2):
            nat[slot, i] = rx[slot, 1 + i].T

    naturals(0)

    def forward(n, slot):
        q0 = n * QB
        nk = min(2 * n + 3, 8)
        kl = nk * BLK
        qt = rx[slot, 0, :, q0:q0 + QB]
        lim = lim_ref[:, q0:q0 + QB]
        peak = jnp.full((8, QB), -1e30, F32)
        for kc in range(nk):
            rows = slice(kc * BLK, (kc + 1) * BLK)
            sc = mm(nat[slot, 0, rows, :], qt, 1, 0)
            if kc * BLK >= q0:
                key = lax.broadcasted_iota(jnp.int32, (BLK, QB), 0) + kc * BLK
                sc = jnp.where(key < lim, sc, -1e30)
            prob[slot, n, rows, :] = sc
            peak = jnp.maximum(peak, jnp.max(sc.reshape(BLK // 8, 8, QB), axis=0))
        peak = jnp.max(peak, axis=0, keepdims=True)
        total = jnp.zeros((8, QB), F32)
        for kc in range(nk):
            rows = slice(kc * BLK, (kc + 1) * BLK)
            ex = jnp.exp2((prob[slot, n, rows, :] - peak) * EXP_SCALE)
            prob[slot, n, rows, :] = ex
            total = total + jnp.sum(ex.reshape(BLK // 8, 8, QB), axis=0)
        total = jnp.sum(total, axis=0, keepdims=True)
        inv = jnp.where(lim > 0, 1.0 / total, 0.0)
        for kc in range(nk):
            rows = slice(kc * BLK, (kc + 1) * BLK)
            wt = prob[slot, n, rows, :] * inv
            prob[slot, n, rows, :] = wt
            low[slot, n, rows, :] = wt.astype(BF)
        ot[slot, :, q0:q0 + QB] = mm(rx[slot, 2, :, :kl], low[slot, n, :kl, :], 1, 0).astype(BF)

    def backward(n, slot):
        q0 = n * QB
        nk = min(2 * n + 3, 8)
        kl = nk * BLK
        qt = rx[slot, 0, :, q0:q0 + QB]
        da = rd[slot, :, q0:q0 + QB]
        delta = jnp.sum(
            da.astype(F32) * ot[slot, :, q0:q0 + QB].astype(F32), axis=0, keepdims=True
        )
        for kc in range(nk):
            rows = slice(kc * BLK, (kc + 1) * BLK)
            dp = mm(nat[slot, 1, rows, :], da, 1, 0)
            dsb[rows, :] = (prob[slot, n, rows, :] * (dp - delta)).astype(BF)
        dqkv[slot, 0, :, q0:q0 + QB] = (mm(rx[slot, 1, :, :kl], dsb[:kl, :], 1, 0) * HD ** (-0.5)).astype(BF)
        acc[slot, 0, :, :kl] += mm(qt, dsb[:kl, :], 1, 1)
        acc[slot, 1, :, :kl] += mm(da, low[slot, n, :kl, :], 1, 1)

    at_remote = []
    for m in range(1, 8):
        b = (s + m) % 8
        at_remote.append(rcopy(ot.at[0, :, lanes(b)], att.at[3 * j + c], s_at.at[m], r_at.at[3 * j + c], clip8 + b))
    at_local = lcopy(ot.at[0, :, lanes(s)], att.at[3 * j + c], r_at.at[3 * j + c])

    def shared_block(n):
        return (1 - c) * (n + 4 * (n // 2)) + c * (n + 2)

    def fwd_item(i, carry):
        slot = i // 4
        qb = jnp.where(i < 4, i, shared_block(2 * (i % 2)) // 2)

        @pl.when(i == 4)
        def _():
            for copy in at_remote:
                copy.start()
            at_local.start()
            wait_shared(xt, rx, r_xc)
            naturals(1)

        for n in range(4):
            @pl.when(qb == n)
            def _(n=n):
                forward(n, slot)

        return carry

    lax.fori_loop(0, 6, fwd_item, 0)

    def shared_send(src, dst, ss, rs, n, block, op):
        @pl.when(block == s)
        def _():
            if op == "start":
                lcopy(src, dst, rs).start()

        @pl.when(block != s)
        def _():
            copy = rcopy(src, dst, ss.at[n], rs, clip8 + block)
            copy.start() if op == "start" else copy.wait_send()

    def atc(op):
        for n in range(4):
            b = shared_block(n)
            shared_send(ot.at[1, :, lanes(b)], att.at[3 * j + 2], s_atc, r_at.at[3 * j + 2], n, b, op)

    atc("start")

    d_fwd = forward_shared(dat, rd, s_df, r_dc)
    wait_shared(dat, rd, r_dc)
    acc[...] = jnp.zeros_like(acc)

    half_there = pl.ds(pl.multiple_of((1 - c) * 512, BLK), 512)
    half_here = pl.ds(pl.multiple_of(c * 512, BLK), 512)
    xc_copy = rcopy(acc.at[1, :, :, half_there], xc, s_xc.at[0], r_xc2.at[0], sib)

    def oq(op):
        for n in range(4):
            b = shared_block(n)
            shared_send(dqkv.at[1, 0, :, lanes(b)], rout.at[3 * j + 2, 0], s_oq, r_oq.at[3 * j + 2], n, b, op)

    def bwd_item(i, carry):
        slot = jnp.where(i < 2, 1, 0)
        qb = jnp.where(i < 2, shared_block(2 * (i % 2)) // 2, i - 2)

        @pl.when(i == 2)
        def _():
            xc_copy.start()
            oq("start")
            wait_own(dat, rd, r_da, r_dc)

        for n in range(4):
            @pl.when(qb == n)
            def _(n=n):
                backward(n, slot)

        return carry

    lax.fori_loop(0, 2, bwd_item, 0)
    for h in range(12):
        lcopy(att.at[0], att.at[h], r_at.at[h]).wait()
    for t in range(6):
        tile = att[2 * t:2 * t + 2].reshape(BLK, BLK).T
        attn[t // 3, :, (t % 3) * BLK:(t % 3 + 1) * BLK] = tile
    ay_remote = []
    for m in range(1, 8):
        p = (pos + m) % 8
        ay_remote.append(
            rcopy(attn.at[p % 2], ay.at[pl.ds(pl.multiple_of(pos * BLK, BLK), BLK), :], s_ay.at[m], r_ay.at[pos], ydev(p))
        )
    ay_local = lcopy(attn.at[c], ay.at[pl.ds(pl.multiple_of(pos * BLK, BLK), BLK), :], r_ay.at[pos])
    for copy in ay_remote:
        copy.start()
    ay_local.start()

    def project(half):
        cols = pl.ds(pl.multiple_of(half * FEAT, BLK), FEAT)
        return mm(attn[0], w_ref[:384, cols], 1, 0) + mm(attn[1], w_ref[384:, cols], 1, 0)

    psend[...] = project(1 - hd).astype(BF)
    p_copy = rcopy(psend, precv, s_p.at[0], r_p.at[0], me, 1 - hd)
    p_copy.start()
    pown[...] = project(hd)

    lax.fori_loop(2, 6, bwd_item, 0)
    for i in range(2):
        scale = HD ** (-0.5) if i == 0 else 1.0
        dqkv[0, 1 + i] = (acc[0, i] * scale).astype(BF)
    o_remote = []
    for m in range(1, 8):
        b = (s + m) % 8
        o_remote.append(rcopy(dqkv.at[0, :, :, lanes(b)], rout.at[3 * j + c], s_o.at[m], r_o.at[3 * j + c], clip8 + b))
    o_local = lcopy(dqkv.at[0, :, :, lanes(s)], rout.at[3 * j + c], r_o.at[3 * j + c])
    for copy in o_remote:
        copy.start()
    o_local.start()

    xc_copy.wait_recv()
    for i in range(2):
        scale = HD ** (-0.5) if i == 0 else 1.0
        dkvc[i] = ((acc[1, i, :, half_here] + xc[i]) * scale).astype(BF)

    def okv(op):
        for n in range(4):
            src = dkvc.at[:, :, n * BLK:(n + 1) * BLK]
            shared_send(src, rout.at[3 * j + 2, 1:3], s_okv, r_o.at[3 * j + 2], n, 4 * c + n, op)

    okv("start")

    for p in range(8):
        lcopy(gt.at[:, 0], gy.at[:, :, lanes(p)], r_gy.at[p]).wait()
        lcopy(attn.at[0], ay.at[p * BLK:(p + 1) * BLK, :], r_ay.at[p]).wait()
    for t in range(2):
        part = mm(gy[4 * t:4 * t + 4].reshape(192, SLOTS), ay[...], 1, 0)
        dfull[4 * t:4 * t + 4] = part.reshape(4, 48, 384)
    zs[...] = dfull[...].astype(BF)
    z_remote = []
    for m in range(1, 8):
        zz = (z + m) % 8
        z_remote.append(rcopy(zs.at[zz], rz.at[z], s_z.at[m], r_z.at[z], zdev(zz)))
    for copy in z_remote:
        copy.start()

    p_copy.wait_recv()
    proj_ref[...] = (pown[...] + precv[...].astype(F32)).astype(BF)

    for jj in range(4):
        for cc in range(2):
            lcopy(rout.at[0], rout.at[3 * jj + cc], r_o.at[3 * jj + cc]).wait()
        lcopy(rout.at[0, 0], rout.at[3 * jj + 2, 0], r_oq.at[3 * jj + 2]).wait()
        lcopy(rout.at[0, 1:3], rout.at[3 * jj + 2, 1:3], r_o.at[3 * jj + 2]).wait()
    for i, ref in enumerate((dq_ref, dk_ref, dv_ref)):
        for t in range(6):
            tile = rout[2 * t:2 * t + 2, i].reshape(BLK, BLK)
            ref[:, t * BLK:(t + 1) * BLK] = tile.T

    summed = dfull[z]
    for m in range(1, 8):
        zz = (z + m) % 8
        lcopy(zs.at[0], rz.at[zz], r_z.at[zz]).wait()
        summed = summed + rz[zz].astype(F32)
    fin[...] = summed.reshape(2, 24, 384)
    mine = xl * 2 + c
    f_remote = []
    for m in range(1, 4):
        t = (mine + m) % 4
        f_remote.append(
            rcopy(fin.at[t // 2], rf.at[mine], s_f.at[m], r_f.at[mine], me - mine + t)
        )
    for copy in f_remote:
        copy.start()
    rf[mine] = fin[xl]
    for m in range(1, 4):
        t = (mine + m) % 4
        lcopy(fin.at[0], rf.at[t], r_f.at[t]).wait()
    for cc in range(2):
        both = rf[cc] + rf[2 + cc]
        dw_ref[:, cc * 384:(cc + 1) * 384] = jnp.where(c == 0, both[:12], both[12:]).astype(BF)

    gsend.wait_send()
    for copy in x_remote + d_remote + x_fwd + d_fwd + gy_remote + at_remote + ay_remote + o_remote + z_remote + f_remote:
        copy.wait_send()
    xc_copy.wait_send()
    p_copy.wait_send()
    atc("wait")
    oq("wait")
    okv("wait")


def local(queries, keys, values, w_out, grad_proj, frame_levels):
    vmem = pl.BlockSpec(memory_space=pltpu.VMEM)
    smem = pl.BlockSpec(memory_space=pltpu.SMEM)
    rows = jax.ShapeDtypeStruct((BLK, FEAT), BF)
    dma = lambda n: pltpu.SemaphoreType.DMA((n,))
    scratch = [
        pltpu.VMEM((12, 3, HD, BLK), BF),
        pltpu.VMEM((2, 3, HD, SLOTS), BF),
        pltpu.VMEM((12, HD, BLK), BF),
        pltpu.VMEM((2, HD, SLOTS), BF),
        pltpu.VMEM((BLK, WIDTH), BF),
        pltpu.VMEM((8, 4, 48, BLK), BF),
        pltpu.VMEM((8, 48, SLOTS), BF),
        pltpu.VMEM((2, 2, SLOTS, HD), BF),
        pltpu.VMEM((1, SLOTS), jnp.int32),
        pltpu.VMEM((2, 4, SLOTS, QB), F32),
        pltpu.VMEM((2, 4, SLOTS, QB), BF),
        pltpu.VMEM((SLOTS, QB), BF),
        pltpu.VMEM((2, HD, SLOTS), BF),
        pltpu.VMEM((12, HD, BLK), BF),
        pltpu.VMEM((2, BLK, 384), BF),
        pltpu.VMEM((BLK, FEAT), F32),
        pltpu.VMEM((BLK, FEAT), BF),
        pltpu.VMEM((BLK, FEAT), BF),
        pltpu.VMEM((2, 2, HD, SLOTS), F32),
        pltpu.VMEM((2, HD, 512), F32),
        pltpu.VMEM((2, 3, HD, SLOTS), BF),
        pltpu.VMEM((2, HD, 512), BF),
        pltpu.VMEM((12, 3, HD, BLK), BF),
        pltpu.VMEM((SLOTS, 384), BF),
        pltpu.VMEM((8, 48, 384), F32),
        pltpu.VMEM((8, 48, 384), BF),
        pltpu.VMEM((8, 48, 384), BF),
        pltpu.VMEM((2, 24, 384), F32),
        pltpu.VMEM((4, 24, 384), F32),
    ] + [
        dma(n)
        for n in (
            11, 3, 8, 8, 11, 3, 8, 8, 2, 1, 8, 8,
            8, 4, 12, 8, 8, 1, 1, 1, 1, 8, 4, 4, 12, 12,
            8, 8, 4, 4,
        )
    ]
    proj, dq, dk, dv, dw = pl.pallas_call(
        kernel,
        out_shape=(rows, rows, rows, rows, jax.ShapeDtypeStruct((12, FEAT), BF)),
        in_specs=[vmem] * 5 + [smem],
        out_specs=[vmem] * 5,
        scratch_shapes=scratch,
        compiler_params=pltpu.CompilerParams(
            collective_id=0, has_side_effects=True, vmem_limit_bytes=56 * 1024 * 1024
        ),
    )(queries, keys, values, w_out, grad_proj, frame_levels)
    return proj, dq, dk, dv, dw.T


def solution(mesh):
    rows = P("frame", "head")
    return jax.shard_map(
        local,
        mesh=mesh,
        in_specs=(rows, rows, rows, P("head", None), rows, P()),
        out_specs=(rows, rows, rows, rows, P("head", "frame")),
        check_vma=False,
    )
```

```python
import functools
import math

import jax
import jax.numpy as jnp
from jax import lax
from jax.experimental import pallas as pl
from jax.experimental.pallas import tpu as pltpu
from jax.sharding import PartitionSpec as P

MESH = pl.DeviceIdType.MESH
BF = jnp.bfloat16
F32 = jnp.float32
HD = 64
BLK = 128
QB = 256
SLOTS = 1024
FEAT = 768
WIDTH = 1536
FRAMES_CLIP = 16
EXP_SCALE = HD ** (-0.5) * math.log2(math.e)


def mm(left, right, dl, dr):
    return lax.dot_general(left, right, (((dl,), (dr,)), ((), ())), preferred_element_type=F32)


def lanes(block):
    return pl.ds(pl.multiple_of(block * BLK, BLK), BLK)


def kernel(
    q_hbm, k_hbm, v_hbm, w_hbm, g_hbm, lev_ref,
    proj_ref, dq_ref, dk_ref, dv_ref, dw_ref,
    q_ref, k_ref, v_ref, w_ref, g_ref, s_in, xt, rx, dat, rd, gfull, gt, gy, nat, lim_ref, prob, low, dsb,
    ot, att, attn, pown, psend, precv, acc, xc, dqkv, dkvc, rout,
    dpart, ay0, ay1, df0, df1, zs0, zs1, rz0, rz1, fin0, fin1, rf0, rf1,
    s_x, s_xf, r_xa, r_xc, s_d, s_df, r_da, r_dc, s_g, r_g, s_gy, r_gy,
    s_at, s_atc, r_at, s_ay, r_ay, s_p, r_p, s_xc, r_xc2, s_o, s_oq, s_okv, r_o, r_oq,
    s_z, r_z, s_f, r_f,
):
    me = lax.axis_index("frame")
    hd = lax.axis_index("head")
    c = me % 2
    xl = (me // 2) % 2
    y = (me // 4) % 4
    z = me // 16
    s = me % 8
    clip8 = me - s
    j = s // 2
    sib = me + 1 - 2 * c
    far_y = 3 - y
    group = y // 2
    pos = group * 2 + c
    others = (3 - j, j + 1 - 2 * (j % 2), (j + 2) % 4)

    def rcopy(src, dst, ss, rs, dev, head=hd):
        return pltpu.make_async_remote_copy(
            src_ref=src, dst_ref=dst, send_sem=ss, recv_sem=rs,
            device_id=(dev, head), device_id_type=MESH,
        )

    def lcopy(src, dst, sem):
        return pltpu.make_async_copy(src, dst, sem)

    def ydev(core):
        return z * 16 + far_y * 4 + xl * 2 + core

    def zdev(zz):
        return zz * 16 + me % 16

    loads = [
        lcopy(src, dst, s_in.at[i])
        for i, (src, dst) in enumerate(
            ((q_hbm, q_ref), (k_hbm, k_ref), (v_hbm, v_ref), (g_hbm, g_ref), (w_hbm, w_ref))
        )
    ]
    for copy in loads:
        copy.start()

    bar = pltpu.get_barrier_semaphore()
    for d in range(1, 8):
        pl.semaphore_signal(bar, inc=1, device_id=(clip8 + (s + d) % 8, hd), device_id_type=MESH)
        pl.semaphore_signal(bar, inc=1, device_id=(zdev((z + d) % 8), hd), device_id_type=MESH)
    pl.semaphore_signal(bar, inc=1, device_id=(me, 1 - hd), device_id_type=MESH)
    for core in range(2):
        pl.semaphore_signal(bar, inc=1, device_id=(ydev(core), hd), device_id_type=MESH)

    for i, ref in enumerate((q_ref, k_ref, v_ref)):
        loads[i].wait()
        for t in range(6):
            tile = ref[:, t * BLK:(t + 1) * BLK].T
            xt[2 * t, i] = tile[:HD]
            xt[2 * t + 1, i] = tile[HD:]
    pl.semaphore_wait(bar, 17)

    def scatter_plan(src, dst, ss, ra, rc):
        remote = []
        shared = []
        for n, jj in enumerate(others):
            base = clip8 + jj * 2
            remote.append(rcopy(src.at[3 * jj], dst.at[0, ..., lanes(s)], ss.at[3 * n], ra.at[s], base))
            remote.append(rcopy(src.at[3 * jj + 1], dst.at[0, ..., lanes(s)], ss.at[3 * n + 1], ra.at[s], base + 1))
            shared.append(rcopy(src.at[3 * jj + 2], dst.at[1, ..., lanes(s)], ss.at[3 * n + 2], rc.at[s], base + c))
        remote.append(rcopy(src.at[3 * j + 1 - c], dst.at[0, ..., lanes(s)], ss.at[9], ra.at[s], sib))
        shared.append(rcopy(src.at[3 * j + 2], dst.at[1, ..., lanes(s)], ss.at[10], rc.at[s], sib))
        local = [
            lcopy(src.at[3 * j + c], dst.at[0, ..., lanes(s)], ra.at[s]),
            lcopy(src.at[3 * j + 2], dst.at[1, ..., lanes(s)], rc.at[s]),
        ]
        return remote + shared, local

    def wait_own(src, dst, ra, rc):
        for b in range(8):
            lcopy(src.at[0], dst.at[0, ..., lanes(b)], ra.at[b]).wait()

    def shared_plan(dst, fs, rc):
        return [
            rcopy(dst.at[1, ..., lanes(jj * 2 + c)], dst.at[1, ..., lanes(jj * 2 + c)], fs.at[n], rc.at[jj * 2 + c], sib)
            for n, jj in enumerate(others)
        ]

    def forward_shared(src, dst, fs, rc):
        for copy, jj in zip(shared_plan(dst, fs, rc), others):
            lcopy(src.at[0], dst.at[1, ..., lanes(jj * 2 + c)], rc.at[jj * 2 + c]).wait()
            copy.start()
        lcopy(src.at[0], dst.at[1, ..., lanes(s)], rc.at[s]).wait()

    def wait_shared(src, dst, rc):
        for jj in range(4):
            b = jj * 2 + 1 - c
            lcopy(src.at[0], dst.at[1, ..., lanes(b)], rc.at[b]).wait()

    x_remote, x_local = scatter_plan(xt, rx, s_x, r_xa, r_xc)
    for copy in x_remote + x_local:
        copy.start()

    slot_iota = lax.broadcasted_iota(jnp.int32, (1, SLOTS), 1)
    seen = jnp.zeros((1, SLOTS), jnp.int32)
    start = jnp.int32(0)
    for f in range(FRAMES_CLIP):
        level = lev_ref[(me // 8) * FRAMES_CLIP + f]
        end = start + jnp.where(level == 0, BLK, jnp.where(level == 1, BLK // 4, BLK // 16))
        seen = jnp.where((slot_iota >= start) & (slot_iota < end), end, seen)
        start = end
    lim_ref[...] = seen

    def transposed_half(half):
        for t in range(6):
            cols = pl.ds(pl.multiple_of(half * FEAT + t * BLK, BLK), BLK)
            tile = gfull[:, cols].T
            for n in range(8):
                row = t * BLK + n * 16
                gt[4 * half + row // 192, (row % 192) // 48, row % 48:row % 48 + 16, :] = tile[n * 16:(n + 1) * 16]

    def gt_part(half, which_group):
        return gt.at[pl.ds(4 * half, 4), pl.ds(2 * which_group, 2)]

    def gy_part(half, p):
        return gy.at[pl.ds(4 * half, 4), :, :, lanes(p)]

    def gy_plan(half, which):
        return [
            rcopy(gt_part(half, 1 - group), gy_part(half, pos), s_gy.at[which, 0], r_gy.at[which, pos], ydev(c)),
            rcopy(gt_part(half, group), gy_part(half, pos), s_gy.at[which, 1], r_gy.at[which, pos], sib),
            lcopy(gt_part(half, group), gy_part(half, pos), r_gy.at[which, pos]),
        ]

    def gy_wait(half, which, p):
        lcopy(gt_part(half, group), gy_part(half, p), r_gy.at[which, p]).wait()

    def gy_forward(half, which):
        p = (1 - group) * 2 + c
        gy_wait(half, which, p)
        copy = rcopy(gy_part(half, p), gy_part(half, p), s_gy.at[which, 2], r_gy.at[which, p], sib)
        copy.start()
        return [copy]

    loads[3].wait()
    own_cols = pl.ds(pl.multiple_of(hd * FEAT, BLK), FEAT)
    gfull[:, own_cols] = g_ref[...]
    transposed_half(hd)
    loads[4].wait()
    for t in range(3):
        dpart[t * QB:(t + 1) * QB, :] = mm(w_ref[t * QB:(t + 1) * QB, own_cols], g_ref[...], 1, 1)
    for copy in x_remote:
        copy.wait_send()
    gsend = rcopy(g_ref, gfull.at[:, own_cols], s_g.at[0], r_g.at[0], me, 1 - hd)
    gsend.start()
    gy_near = gy_plan(hd, 0)
    for copy in gy_near:
        copy.start()
    wait_own(xt, rx, r_xa, r_xc)

    def naturals(slot):
        for i in range(2):
            nat[slot, i] = rx[slot, 1 + i].T

    naturals(0)

    def forward(n, slot):
        q0 = n * QB
        nk = min(2 * n + 3, 8)
        kl = nk * BLK
        qt = rx[slot, 0, :, q0:q0 + QB]
        lim = lim_ref[:, q0:q0 + QB]
        peak = jnp.full((8, QB), -1e30, F32)
        for kc in range(nk):
            rows = slice(kc * BLK, (kc + 1) * BLK)
            sc = mm(nat[slot, 0, rows, :], qt, 1, 0)
            if kc * BLK >= q0:
                key = lax.broadcasted_iota(jnp.int32, (BLK, QB), 0) + kc * BLK
                sc = jnp.where(key < lim, sc, -1e30)
            prob[slot, n, rows, :] = sc
            peak = jnp.maximum(peak, jnp.max(sc.reshape(BLK // 8, 8, QB), axis=0))
        peak = jnp.max(peak, axis=0, keepdims=True)
        total = jnp.zeros((8, QB), F32)
        for kc in range(nk):
            rows = slice(kc * BLK, (kc + 1) * BLK)
            ex = jnp.exp2((prob[slot, n, rows, :] - peak) * EXP_SCALE)
            prob[slot, n, rows, :] = ex
            total = total + jnp.sum(ex.reshape(BLK // 8, 8, QB), axis=0)
        total = jnp.sum(total, axis=0, keepdims=True)
        inv = jnp.where(lim > 0, 1.0 / total, 0.0)
        for kc in range(nk):
            rows = slice(kc * BLK, (kc + 1) * BLK)
            wt = prob[slot, n, rows, :] * inv
            prob[slot, n, rows, :] = wt
            low[slot, n, rows, :] = wt.astype(BF)
        ot[slot, :, q0:q0 + QB] = mm(rx[slot, 2, :, :kl], low[slot, n, :kl, :], 1, 0).astype(BF)

    def backward(n, slot):
        q0 = n * QB
        nk = min(2 * n + 3, 8)
        kl = nk * BLK
        qt = rx[slot, 0, :, q0:q0 + QB]
        da = rd[slot, :, q0:q0 + QB]
        delta = jnp.sum(
            da.astype(F32) * ot[slot, :, q0:q0 + QB].astype(F32), axis=0, keepdims=True
        )
        for kc in range(nk):
            rows = slice(kc * BLK, (kc + 1) * BLK)
            dp = mm(nat[slot, 1, rows, :], da, 1, 0)
            dsb[rows, :] = (prob[slot, n, rows, :] * (dp - delta)).astype(BF)
        dqkv[slot, 0, :, q0:q0 + QB] = (mm(rx[slot, 1, :, :kl], dsb[:kl, :], 1, 0) * HD ** (-0.5)).astype(BF)
        acc[slot, 0, :, :kl] += mm(qt, dsb[:kl, :], 1, 1)
        acc[slot, 1, :, :kl] += mm(da, low[slot, n, :kl, :], 1, 1)

    at_remote = []
    for m in range(1, 8):
        b = (s + m) % 8
        at_remote.append(rcopy(ot.at[0, :, lanes(b)], att.at[3 * j + c], s_at.at[m], r_at.at[3 * j + c], clip8 + b))
    at_local = lcopy(ot.at[0, :, lanes(s)], att.at[3 * j + c], r_at.at[3 * j + c])

    def shared_block(n):
        return (1 - c) * (n + 4 * (n // 2)) + c * (n + 2)

    def fwd_item(i, carry):
        slot = i // 4
        qb = jnp.where(i < 4, i, shared_block(2 * (i % 2)) // 2)

        @pl.when(i == 2)
        def _():
            forward_shared(xt, rx, s_xf, r_xc)

        @pl.when(i == 4)
        def _():
            for copy in at_remote:
                copy.start()
            at_local.start()
            wait_shared(xt, rx, r_xc)
            naturals(1)

        for n in range(4):
            @pl.when(qb == n)
            def _(n=n):
                forward(n, slot)

        return carry

    lax.fori_loop(0, 6, fwd_item, 0)

    def shared_send(src, dst, ss, rs, n, block, op):
        @pl.when(block == s)
        def _():
            if op == "start":
                lcopy(src, dst, rs).start()

        @pl.when(block != s)
        def _():
            copy = rcopy(src, dst, ss.at[n], rs, clip8 + block)
            copy.start() if op == "start" else copy.wait_send()

    def atc(op):
        for n in range(4):
            b = shared_block(n)
            shared_send(ot.at[1, :, lanes(b)], att.at[3 * j + 2], s_atc, r_at.at[3 * j + 2], n, b, op)

    atc("start")

    gsend.wait_recv()
    other_cols = pl.ds(pl.multiple_of((1 - hd) * FEAT, BLK), FEAT)
    for t in range(3):
        rows = slice(t * QB, (t + 1) * QB)
        part = (dpart[rows, :] + mm(w_ref[rows, other_cols], gfull[:, other_cols], 1, 1)).astype(BF)
        for n in range(4):
            dat[4 * t + n] = part[n * HD:(n + 1) * HD]
    d_remote, d_local = scatter_plan(dat, rd, s_d, r_da, r_dc)
    for copy in d_remote + d_local:
        copy.start()
    gy_far_fwd = gy_forward(hd, 0)
    transposed_half(1 - hd)
    gy_far = gy_plan(1 - hd, 1)
    for copy in gy_far:
        copy.start()
    acc[...] = jnp.zeros_like(acc)

    half_there = pl.ds(pl.multiple_of((1 - c) * 512, BLK), 512)
    half_here = pl.ds(pl.multiple_of(c * 512, BLK), 512)
    xc_copy = rcopy(acc.at[1, :, :, half_there], xc, s_xc.at[0], r_xc2.at[0], sib)

    def oq(op):
        for n in range(4):
            b = shared_block(n)
            shared_send(dqkv.at[1, 0, :, lanes(b)], rout.at[3 * j + 2, 0], s_oq, r_oq.at[3 * j + 2], n, b, op)

    ready = {3: (), 2: (5, 6, 7), 1: (3, 4), 0: (0, 1, 2)}

    def own_send(b, op):
        shared_send(dqkv.at[0, :, :, lanes(b)], rout.at[3 * j + c], s_o, r_o.at[3 * j + c], b, b, op)

    def finish(n):
        if not ready[n]:
            return
        span = slice(ready[n][0] * BLK, (ready[n][-1] + 1) * BLK)
        dqkv[0, 1, :, span] = (acc[0, 0, :, span] * HD ** (-0.5)).astype(BF)
        dqkv[0, 2, :, span] = acc[0, 1, :, span].astype(BF)
        for b in ready[n]:
            own_send(b, "start")

    def bwd_item(i, carry):
        slot = jnp.where(i < 2, 1, 0)
        qb = jnp.where(i < 2, shared_block(2 * (i % 2)) // 2, 5 - i)

        @pl.when(i == 2)
        def _():
            xc_copy.start()
            oq("start")
            wait_own(dat, rd, r_da, r_dc)

        for n in range(4):
            @pl.when(qb == n)
            def _(n=n):
                backward(n, slot)

                @pl.when(slot == 0)
                def _():
                    finish(n)

        return carry

    ay_remote = []
    for part, tiles in enumerate(((0,), (1, 2))):
        for core in range(2):
            for t in tiles:
                t = 3 * core + t
                for h in (2 * t, 2 * t + 1):
                    lcopy(att.at[0], att.at[h], r_at.at[h]).wait()
                tile = att[2 * t:2 * t + 2].reshape(BLK, BLK).T
                attn[core, :, (t % 3) * BLK:(t % 3 + 1) * BLK] = tile
        cols = pl.ds(tiles[0] * BLK, len(tiles) * BLK)
        rows = pl.ds(pl.multiple_of(pos * BLK, BLK), BLK)
        dst = (ay0, ay1)[part].at[rows, :]
        for n, (core, dev) in enumerate(((0, ydev(0)), (1, ydev(1)), (1 - c, sib))):
            ay_remote.append(rcopy(attn.at[core, :, cols], dst, s_ay.at[part, n], r_ay.at[part, pos], dev))
            ay_remote[-1].start()
        lcopy(attn.at[c, :, cols], dst, r_ay.at[part, pos]).start()

    def project(half):
        cols = pl.ds(pl.multiple_of(half * FEAT, BLK), FEAT)
        return mm(attn[0], w_ref[:384, cols], 1, 0) + mm(attn[1], w_ref[384:, cols], 1, 0)

    psend[...] = project(1 - hd).astype(BF)
    p_copy = rcopy(psend, precv, s_p.at[0], r_p.at[0], me, 1 - hd)
    p_copy.start()
    pown[...] = project(hd)

    forward_shared(dat, rd, s_df, r_dc)
    wait_shared(dat, rd, r_dc)
    lax.fori_loop(0, 2, bwd_item, 0)
    gy_far_fwd += gy_forward(1 - hd, 1)
    for which, half in ((0, hd), (1, 1 - hd)):
        gy_wait(half, which, pos)
        for g in range(2):
            gy_wait(half, which, g * 2 + 1 - c)
    z_remote = []
    for part, (ayp, dp, zp, rzp) in enumerate(((ay0, df0, zs0, rz0), (ay1, df1, zs1, rz1))):
        for p in range(4):
            rows = pl.ds(p * BLK, BLK)
            lcopy(ayp.at[rows, :], ayp.at[rows, :], r_ay.at[part, p]).wait()
        for t in range(2):
            sums = mm(gy[4 * t:4 * t + 4].reshape(384, 512), ayp[...], 1, 0)
            sums = sums.reshape(4, 96, sums.shape[1])
            dp[4 * t:4 * t + 4] = sums
            zp[4 * t:4 * t + 4] = sums.astype(BF)
        for m in range(1, 8):
            zz = (z + m) % 8
            z_remote.append(rcopy(zp.at[zz], rzp.at[z], s_z.at[part, m], r_z.at[part, z], zdev(zz)))
            z_remote[-1].start()

    lax.fori_loop(2, 6, bwd_item, 0)
    xc_copy.wait_recv()
    for i in range(2):
        scale = HD ** (-0.5) if i == 0 else 1.0
        dkvc[i] = ((acc[1, i, :, half_here] + xc[i]) * scale).astype(BF)

    def okv(op):
        for n in range(4):
            src = dkvc.at[:, :, n * BLK:(n + 1) * BLK]
            shared_send(src, rout.at[3 * j + 2, 1:3], s_okv, r_o.at[3 * j + 2], n, 4 * c + n, op)

    okv("start")

    p_copy.wait_recv()
    proj_ref[...] = (pown[...] + precv[...].astype(F32)).astype(BF)

    for jj in range(4):
        for cc in range(2):
            lcopy(rout.at[0], rout.at[3 * jj + cc], r_o.at[3 * jj + cc]).wait()
        lcopy(rout.at[0, 0], rout.at[3 * jj + 2, 0], r_oq.at[3 * jj + 2]).wait()
        lcopy(rout.at[0, 1:3], rout.at[3 * jj + 2, 1:3], r_o.at[3 * jj + 2]).wait()
    for i, ref in enumerate((dq_ref, dk_ref, dv_ref)):
        for t in range(6):
            tile = rout[2 * t:2 * t + 2, i].reshape(BLK, BLK)
            ref[:, t * BLK:(t + 1) * BLK] = tile.T

    f_remote = []
    for part, (dp, rzp, fp, rfp) in enumerate(((df0, rz0, fin0, rf0), (df1, rz1, fin1, rf1))):
        summed = dp[z]
        for m in range(1, 8):
            zz = (z + m) % 8
            lcopy(rzp.at[zz], rzp.at[zz], r_z.at[part, zz]).wait()
            summed = summed + rzp[zz].astype(F32)
        for t in range(8):
            fp[t, :12, :] = summed[12 * t:12 * t + 12]
        for m in range(1, 8):
            t = (s + m) % 8
            f_remote.append(rcopy(fp.at[t], rfp.at[s], s_f.at[part, m], r_f.at[part, s], clip8 + t))
            f_remote[-1].start()
        rfp[s] = fp[s]
    for part, (rfp, lo, hi) in enumerate(((rf0, 0, BLK), (rf1, BLK, 3 * BLK))):
        for m in range(1, 8):
            t = (s + m) % 8
            lcopy(rfp.at[t], rfp.at[t], r_f.at[part, t]).wait()
        for core in range(2):
            every = rfp[core] + rfp[2 + core] + rfp[4 + core] + rfp[6 + core]
            dw_ref[:, core * 384 + lo:core * 384 + hi] = every[:12].astype(BF)

    gsend.wait_send()
    for copy in d_remote + shared_plan(rx, s_xf, r_xc) + shared_plan(rd, s_df, r_dc) + gy_near[:2] + gy_far[:2] + gy_far_fwd + at_remote + ay_remote + z_remote + f_remote:
        copy.wait_send()
    xc_copy.wait_send()
    p_copy.wait_send()
    atc("wait")
    oq("wait")
    for b in range(8):
        own_send(b, "wait")
    okv("wait")


def place(*refs):
    for i in range(5):
        refs[5 + i][...] = refs[i][...]


def local(queries, keys, values, w_out, grad_proj, frame_levels):
    vmem = pl.BlockSpec(memory_space=pltpu.VMEM)
    smem = pl.BlockSpec(memory_space=pltpu.SMEM)
    hbm = pl.BlockSpec(memory_space=pl.ANY)
    rows = jax.ShapeDtypeStruct((BLK, FEAT), BF)
    dma = lambda n: pltpu.SemaphoreType.DMA(n if isinstance(n, tuple) else (n,))
    scratch = [pltpu.VMEM((BLK, FEAT), BF)] * 3 + [
        pltpu.VMEM((FEAT, WIDTH), BF),
        pltpu.VMEM((BLK, FEAT), BF),
        dma(5),
        pltpu.VMEM((12, 3, HD, BLK), BF),
        pltpu.VMEM((2, 3, HD, SLOTS), BF),
        pltpu.VMEM((12, HD, BLK), BF),
        pltpu.VMEM((2, HD, SLOTS), BF),
        pltpu.VMEM((BLK, WIDTH), BF),
        pltpu.VMEM((8, 4, 48, BLK), BF),
        pltpu.VMEM((8, 2, 48, 512), BF),
        pltpu.VMEM((2, 2, SLOTS, HD), BF),
        pltpu.VMEM((1, SLOTS), jnp.int32),
        pltpu.VMEM((2, 4, SLOTS, QB), F32),
        pltpu.VMEM((2, 4, SLOTS, QB), BF),
        pltpu.VMEM((SLOTS, QB), BF),
        pltpu.VMEM((2, HD, SLOTS), BF),
        pltpu.VMEM((12, HD, BLK), BF),
        pltpu.VMEM((2, BLK, 384), BF),
        pltpu.VMEM((BLK, FEAT), F32),
        pltpu.VMEM((BLK, FEAT), BF),
        pltpu.VMEM((BLK, FEAT), BF),
        pltpu.VMEM((2, 2, HD, SLOTS), F32),
        pltpu.VMEM((2, HD, 512), F32),
        pltpu.VMEM((2, 3, HD, SLOTS), BF),
        pltpu.VMEM((2, HD, 512), BF),
        pltpu.VMEM((12, 3, HD, BLK), BF),
        pltpu.VMEM((FEAT, BLK), F32),
    ] + [
        pltpu.VMEM(lead + (n * BLK,), kind)
        for lead, kind in (
            ((512,), BF),
            ((8, 96), F32),
            ((8, 96), BF),
            ((8, 96), BF),
            ((8, 16), F32),
            ((8, 16), F32),
        )
        for n in (1, 2)
    ] + [
        dma(n)
        for n in (
            11, 3, 8, 8, 11, 3, 8, 8, 1, 1, (2, 3), (2, 4),
            8, 4, 12, (2, 3), (2, 4), 1, 1, 1, 1, 8, 4, 4, 12, 12,
            (2, 8), (2, 8), (2, 8), (2, 8),
        )
    ]
    proj, dq, dk, dv, dw = pl.pallas_call(
        kernel,
        out_shape=(rows, rows, rows, rows, jax.ShapeDtypeStruct((12, FEAT), BF)),
        in_specs=[hbm] * 5 + [smem],
        out_specs=[vmem] * 5,
        scratch_shapes=scratch,
        compiler_params=pltpu.CompilerParams(
            collective_id=0, has_side_effects=True, vmem_limit_bytes=56 * 1024 * 1024
        ),
    )(queries, keys, values, w_out, grad_proj, frame_levels)
    strict = pl.BlockSpec(memory_space=pltpu.HBM)
    proj, dq, dk, dv, dw = pl.pallas_call(
        place,
        out_shape=(rows,) * 4 + (jax.ShapeDtypeStruct((12, FEAT), BF),),
        in_specs=[vmem] * 5,
        out_specs=[vmem] * 5,
        scratch_shapes=[],
    )(proj, dq, dk, dv, dw)
    return proj, dq, dk, dv, dw.T


def solution(mesh):
    rows = P("frame", "head")
    return jax.shard_map(
        local,
        mesh=mesh,
        in_specs=(rows, rows, rows, P("head", None), rows, P()),
        out_specs=(rows, rows, rows, rows, P("head", "frame")),
        check_vma=False,
    )
```

```python
import functools
import math

import jax
import jax.numpy as jnp
from jax import lax
from jax.experimental import pallas as pl
from jax.experimental.pallas import tpu as pltpu
from jax.sharding import PartitionSpec as P

MESH = pl.DeviceIdType.MESH
BF = jnp.bfloat16
F32 = jnp.float32
HD = 64
BLK = 128
QB = 256
SLOTS = 1024
FEAT = 768
WIDTH = 1536
FRAMES_CLIP = 16
EXP_SCALE = HD ** (-0.5) * math.log2(math.e)


def mm(left, right, dl, dr):
    return lax.dot_general(left, right, (((dl,), (dr,)), ((), ())), preferred_element_type=F32)


def lanes(block):
    return pl.ds(pl.multiple_of(block * BLK, BLK), BLK)


def kernel(
    q_hbm, k_hbm, v_hbm, w_hbm, g_hbm, lev_ref,
    proj_hbm, dq_hbm, dk_hbm, dv_hbm, dw_ref,
    proj_ref, dq_ref, dk_ref, dv_ref, s_out, q_ref, k_ref, v_ref, w_ref, g_ref, s_in, xt, rx, dat, rd, gfull, gt, gy, nat, lim_ref, inv_ref, prob, low, dsb,
    ot, att, attn, pown, psend, precv, acc, xc, dqkv, dkvc, rout,
    dpart, ayt, df, zs, rz, fin, rf,
    s_x, s_xf, r_xa, r_xc, s_d, s_df, r_da, r_dc, s_g, r_g, s_gy, r_gy,
    s_at, r_at, s_ay, r_ay, s_p, r_p, s_xc, r_xc2, s_o, s_oq, s_okv, r_o, r_oq,
    s_z, r_z, s_f, r_f,
):
    me = lax.axis_index("frame")
    hd = lax.axis_index("head")
    c = me % 2
    xl = (me // 2) % 2
    y = (me // 4) % 4
    z = me // 16
    s = me % 8
    clip8 = me - s
    j = s // 2
    sib = me + 1 - 2 * c
    far_y = 3 - y
    group = y // 2
    pos = group * 2 + c
    others = (3 - j, j + 1 - 2 * (j % 2), (j + 2) % 4)

    def rcopy(src, dst, ss, rs, dev, head=hd):
        return pltpu.make_async_remote_copy(
            src_ref=src, dst_ref=dst, send_sem=ss, recv_sem=rs,
            device_id=(dev, head), device_id_type=MESH,
        )

    def lcopy(src, dst, sem):
        return pltpu.make_async_copy(src, dst, sem)

    def ydev(core):
        return z * 16 + far_y * 4 + xl * 2 + core

    def zdev(zz):
        return zz * 16 + me % 16

    loads = [
        lcopy(src, dst, s_in.at[i])
        for i, (src, dst) in enumerate(
            ((q_hbm, q_ref), (k_hbm, k_ref), (v_hbm, v_ref), (g_hbm, g_ref), (w_hbm, w_ref))
        )
    ]
    for copy in loads:
        copy.start()

    bar = pltpu.get_barrier_semaphore()
    for d in range(1, 8):
        pl.semaphore_signal(bar, inc=1, device_id=(clip8 + (s + d) % 8, hd), device_id_type=MESH)
    pl.semaphore_signal(bar, inc=1, device_id=(me, 1 - hd), device_id_type=MESH)
    for core in range(2):
        pl.semaphore_signal(bar, inc=1, device_id=(ydev(core), hd), device_id_type=MESH)
    for d in (1, 2, 6, 7):
        pl.semaphore_signal(bar, inc=1, device_id=(zdev((z + d) % 8), hd), device_id_type=MESH)

    for i, ref in enumerate((q_ref, k_ref, v_ref)):
        loads[i].wait()
        for t in range(6):
            tile = ref[:, t * BLK:(t + 1) * BLK].T
            xt[2 * t, i] = tile[:HD]
            xt[2 * t + 1, i] = tile[HD:]
    pl.semaphore_wait(bar, 14)

    def scatter_plan(src, dst, ss, ra, rc):
        remote = []
        shared = []
        for n, jj in enumerate(others):
            base = clip8 + jj * 2
            remote.append(rcopy(src.at[3 * jj], dst.at[0, ..., lanes(s)], ss.at[3 * n], ra.at[s], base))
            remote.append(rcopy(src.at[3 * jj + 1], dst.at[0, ..., lanes(s)], ss.at[3 * n + 1], ra.at[s], base + 1))
            shared.append(rcopy(src.at[3 * jj + 2], dst.at[1, ..., lanes(s)], ss.at[3 * n + 2], rc.at[s], base + c))
        remote.append(rcopy(src.at[3 * j + 1 - c], dst.at[0, ..., lanes(s)], ss.at[9], ra.at[s], sib))
        shared.append(rcopy(src.at[3 * j + 2], dst.at[1, ..., lanes(s)], ss.at[10], rc.at[s], sib))
        local = [
            lcopy(src.at[3 * j + c], dst.at[0, ..., lanes(s)], ra.at[s]),
            lcopy(src.at[3 * j + 2], dst.at[1, ..., lanes(s)], rc.at[s]),
        ]
        return remote + shared, local

    def wait_own(src, dst, ra, rc):
        for b in range(8):
            lcopy(src.at[0], dst.at[0, ..., lanes(b)], ra.at[b]).wait()

    def shared_plan(dst, fs, rc):
        return [
            rcopy(dst.at[1, ..., lanes(jj * 2 + c)], dst.at[1, ..., lanes(jj * 2 + c)], fs.at[n], rc.at[jj * 2 + c], sib)
            for n, jj in enumerate(others)
        ]

    def forward_shared(src, dst, fs, rc):
        for copy, jj in zip(shared_plan(dst, fs, rc), others):
            lcopy(src.at[0], dst.at[1, ..., lanes(jj * 2 + c)], rc.at[jj * 2 + c]).wait()
            copy.start()
        lcopy(src.at[0], dst.at[1, ..., lanes(s)], rc.at[s]).wait()

    def wait_shared(src, dst, rc):
        for jj in range(4):
            b = jj * 2 + 1 - c
            lcopy(src.at[0], dst.at[1, ..., lanes(b)], rc.at[b]).wait()

    x_remote, x_local = scatter_plan(xt, rx, s_x, r_xa, r_xc)
    for copy in x_remote + x_local:
        copy.start()

    slot_iota = lax.broadcasted_iota(jnp.int32, (1, SLOTS), 1)
    seen = jnp.zeros((1, SLOTS), jnp.int32)
    start = jnp.int32(0)
    for f in range(FRAMES_CLIP):
        level = lev_ref[(me // 8) * FRAMES_CLIP + f]
        end = start + jnp.where(level == 0, BLK, jnp.where(level == 1, BLK // 4, BLK // 16))
        seen = jnp.where((slot_iota >= start) & (slot_iota < end), end, seen)
        start = end
    lim_ref[...] = seen

    def transposed_half(half):
        for t in range(6):
            cols = pl.ds(pl.multiple_of(half * FEAT + t * BLK, BLK), BLK)
            tile = gfull[:, cols].T
            for n in range(8):
                row = t * BLK + n * 16
                gt[4 * half + row // 192, (row % 192) // 48, row % 48:row % 48 + 16, :] = tile[n * 16:(n + 1) * 16]

    def gt_part(half, which_group):
        return gt.at[pl.ds(4 * half, 4), pl.ds(2 * which_group, 2)]

    def gy_part(half, p):
        return gy.at[pl.ds(4 * half, 4), :, :, lanes(p)]

    def gy_plan(half, which):
        return [
            rcopy(gt_part(half, 1 - group), gy_part(half, pos), s_gy.at[which, 0], r_gy.at[which, pos], ydev(c)),
            rcopy(gt_part(half, group), gy_part(half, pos), s_gy.at[which, 1], r_gy.at[which, pos], sib),
            lcopy(gt_part(half, group), gy_part(half, pos), r_gy.at[which, pos]),
        ]

    def gy_wait(half, which, p):
        lcopy(gt_part(half, group), gy_part(half, p), r_gy.at[which, p]).wait()

    def gy_forward(half, which):
        p = (1 - group) * 2 + c
        gy_wait(half, which, p)
        copy = rcopy(gy_part(half, p), gy_part(half, p), s_gy.at[which, 2], r_gy.at[which, p], sib)
        copy.start()
        return [copy]

    loads[3].wait()
    own_cols = pl.ds(pl.multiple_of(hd * FEAT, BLK), FEAT)
    gfull[:, own_cols] = g_ref[...]
    transposed_half(hd)
    loads[4].wait()
    for t in range(3):
        dpart[t * QB:(t + 1) * QB, :] = mm(w_ref[t * QB:(t + 1) * QB, own_cols], g_ref[...], 1, 1)
    for copy in x_remote:
        copy.wait_send()
    gsend = rcopy(g_ref, gfull.at[:, own_cols], s_g.at[0], r_g.at[0], me, 1 - hd)
    gsend.start()
    gy_near = gy_plan(hd, 0)
    for copy in gy_near:
        copy.start()
    wait_own(xt, rx, r_xa, r_xc)

    def naturals(slot):
        for i in range(2):
            nat[slot, i] = rx[slot, 1 + i].T

    naturals(0)

    def forward(ns, slot):
        q0s = [n * QB for n in ns]
        nks = [min(2 * n + 3, 8) for n in ns]
        qts = [rx[slot, 0, :, q0:q0 + QB] for q0 in q0s]
        lims = [lim_ref[:, q0:q0 + QB] for q0 in q0s]
        peaks = [jnp.full((8, QB), -1e30, F32) for _ in ns]
        work = [(kc, p) for kc in range(8) for p in range(2) if kc < nks[p]]
        for kc, p in work:
            rows = slice(kc * BLK, (kc + 1) * BLK)
            sc = mm(nat[slot, 0, rows, :], qts[p], 1, 0)
            if kc * BLK >= q0s[p]:
                key = lax.broadcasted_iota(jnp.int32, (BLK, QB), 0) + kc * BLK
                sc = jnp.where(key < lims[p], sc, -1e30)
            prob[slot, ns[p], rows, :] = sc
            peaks[p] = jnp.maximum(peaks[p], jnp.max(sc.reshape(BLK // 8, 8, QB), axis=0))
        peaks = [jnp.max(peak, axis=0, keepdims=True) for peak in peaks]
        totals = [jnp.zeros((8, QB), F32) for _ in ns]
        for kc, p in work:
            rows = slice(kc * BLK, (kc + 1) * BLK)
            ex = jnp.exp2((prob[slot, ns[p], rows, :] - peaks[p]) * EXP_SCALE)
            prob[slot, ns[p], rows, :] = ex
            totals[p] = totals[p] + jnp.sum(ex.reshape(BLK // 8, 8, QB), axis=0)
        totals = [jnp.sum(total, axis=0, keepdims=True) for total in totals]
        invs = [jnp.where(lim > 0, 1.0 / total, 0.0) for lim, total in zip(lims, totals)]
        for p in range(2):
            inv_ref[slot, :, q0s[p]:q0s[p] + QB] = invs[p]
        for kc, p in work:
            rows = slice(kc * BLK, (kc + 1) * BLK)
            low[slot, ns[p], rows, :] = (prob[slot, ns[p], rows, :] * invs[p]).astype(BF)
        for p in range(2):
            kl = nks[p] * BLK
            ot[slot, :, q0s[p]:q0s[p] + QB] = mm(rx[slot, 2, :, :kl], low[slot, ns[p], :kl, :], 1, 0).astype(BF)

    def backward(ns, slot):
        q0s = [n * QB for n in ns]
        nks = [min(2 * n + 3, 8) for n in ns]
        qts = [rx[slot, 0, :, q0:q0 + QB] for q0 in q0s]
        das = [rd[slot, :, q0:q0 + QB] for q0 in q0s]
        invs = [inv_ref[slot, :, q0:q0 + QB] for q0 in q0s]
        deltas = [
            jnp.sum(da.astype(F32) * ot[slot, :, q0:q0 + QB].astype(F32), axis=0, keepdims=True)
            for da, q0 in zip(das, q0s)
        ]
        for kc in range(8):
            rows = slice(kc * BLK, (kc + 1) * BLK)
            for p in range(2):
                if kc < nks[p]:
                    dp = mm(nat[slot, 1, rows, :], das[p], 1, 0)
                    dsb[p, rows, :] = (prob[slot, ns[p], rows, :] * invs[p] * (dp - deltas[p])).astype(BF)
        for p in range(2):
            kl = nks[p] * BLK
            dq = mm(rx[slot, 1, :, :kl], dsb[p, :kl, :], 1, 0) * HD ** (-0.5)
            dqkv[slot, 0, :, q0s[p]:q0s[p] + QB] = dq.astype(BF)
        for p in range(2):
            kl = nks[p] * BLK
            acc[slot, 0, :, :kl] += mm(qts[p], dsb[p, :kl, :], 1, 1)
            acc[slot, 1, :, :kl] += mm(das[p], low[slot, ns[p], :kl, :], 1, 1)

    def shared_send(src, dst, ss, rs, n, block, op):
        @pl.when(block == s)
        def _():
            if op == "start":
                lcopy(src, dst, rs).start()

        @pl.when(block != s)
        def _():
            copy = rcopy(src, dst, ss.at[n], rs, clip8 + block)
            copy.start() if op == "start" else copy.wait_send()

    def at_send(slot, n, op):
        head = 3 * j + c + slot * (2 - c)
        for b in (2 * n, 2 * n + 1):
            shared_send(ot.at[slot, :, lanes(b)], att.at[head], s_at.at[slot], r_at.at[head], b, b, op)

    def shared_block(n):
        return (1 - c) * (n + 4 * (n // 2)) + c * (n + 2)

    pairs = ((0, 3), (1, 2))

    def fwd_item(i, carry):
        slot = i // 2
        pair = jnp.where(i < 2, i, c)

        @pl.when(i == 1)
        def _():
            forward_shared(xt, rx, s_xf, r_xc)

        @pl.when(i == 2)
        def _():
            wait_shared(xt, rx, r_xc)
            naturals(1)

        for n in range(2):
            @pl.when(pair == n)
            def _(n=n):
                forward(pairs[n], slot)
                for qb in pairs[n]:
                    at_send(slot, qb, "start")

        return carry

    lax.fori_loop(0, 3, fwd_item, 0)

    acc[...] = jnp.zeros_like(acc)
    half_there = pl.ds(pl.multiple_of((1 - c) * 512, BLK), 512)
    half_here = pl.ds(pl.multiple_of(c * 512, BLK), 512)
    xc_copy = rcopy(acc.at[1, :, :, half_there], xc, s_xc.at[0], r_xc2.at[0], sib)

    def oq(op):
        for n in range(4):
            b = shared_block(n)
            shared_send(dqkv.at[1, 0, :, lanes(b)], rout.at[3 * j + 2, 0], s_oq, r_oq.at[3 * j + 2], n, b, op)

    def okv(op):
        for n in range(4):
            src = dkvc.at[:, :, n * BLK:(n + 1) * BLK]
            shared_send(src, rout.at[3 * j + 2, 1:3], s_okv, r_o.at[3 * j + 2], n, 4 * c + n, op)

    def own_send(b, op):
        shared_send(dqkv.at[0, :, :, lanes(b)], rout.at[3 * j + c], s_o, r_o.at[3 * j + c], b, b, op)

    def finish():
        dqkv[0, 1] = (acc[0, 0] * HD ** (-0.5)).astype(BF)
        dqkv[0, 2] = acc[0, 1].astype(BF)
        for b in range(8):
            own_send(b, "start")

    def bwd_item(i, carry):
        slot = jnp.where(i == 0, 1, 0)
        pair = jnp.where(i == 0, c, i - 1)

        @pl.when(i == 1)
        def _():
            xc_copy.start()
            oq("start")
            wait_own(dat, rd, r_da, r_dc)

        @pl.when(i == 2)
        def _():
            xc_copy.wait_recv()
            for part in range(2):
                scale = HD ** (-0.5) if part == 0 else 1.0
                dkvc[part] = ((acc[1, part, :, half_here] + xc[part]) * scale).astype(BF)
            okv("start")

        for n in range(2):
            @pl.when(pair == n)
            def _(n=n):
                backward(pairs[n], slot)

        return carry

    ay_remote = []

    def attended_part(part):
        for core in range(2):
            for h in range(2):
                lcopy(att.at[0], att.at[6 * core + 2 * part + h], r_at.at[6 * core + 2 * part + h]).wait()
        dst = ayt.at[part, :, :, lanes(pos)]
        for n, (core, dev) in enumerate(((0, ydev(0)), (1, ydev(1)), (1 - c, sib))):
            src = att.at[pl.ds(6 * core + 2 * part, 2)]
            ay_remote.append(rcopy(src, dst, s_ay.at[part, n], r_ay.at[part, pos], dev))
            ay_remote[-1].start()
        lcopy(att.at[pl.ds(6 * c + 2 * part, 2)], dst, r_ay.at[part, pos]).start()

    def attended_rows():
        for t in range(6):
            tile = att[2 * t:2 * t + 2].reshape(BLK, BLK).T
            attn[t // 3, :, (t % 3) * BLK:(t % 3 + 1) * BLK] = tile

    first_hops = ((4, 2, 0), (3, 1, 1), (5, 7, 2), (1, 1, 3), (7, 7, 4))
    second_hops = ((2, 2, 5, (0, 1)), (6, 6, 6, (2,)))

    def z_copy(owner, to, slot):
        return rcopy(zs.at[(z + owner) % 8], rz.at[slot], s_z.at[slot], r_z.at[slot], zdev((z + to) % 8))

    def z_arrived(slot):
        lcopy(rz.at[slot], rz.at[slot], r_z.at[slot]).wait()

    def z_first(half):
        for owner, to, slot in first_hops:
            @pl.when(((z + owner) % 8) // 4 == half)
            def _():
                z_copy(owner, to, slot).start()

    def z_second():
        for owner, to, slot, joined in second_hops:
            piece = df[(z + owner) % 8]
            for n in joined:
                z_arrived(n)
                piece = piece + rz[n].astype(F32)
            zs[(z + owner) % 8] = piece.astype(BF)
            z_copy(owner, to, slot).start()

    def gy_arrived(half, which):
        gy_wait(half, which, pos)
        for g in range(2):
            gy_wait(half, which, g * 2 + 1 - c)

    def ay_arrived(part):
        for p in range(4):
            dst = ayt.at[part, :, :, lanes(p)]
            lcopy(dst, dst, r_ay.at[part, p]).wait()

    def weight_part(part, half):
        mine = pl.ds(4 * half, 4)
        heads = ayt[part].reshape(BLK, 512)
        sums = mm(gy[mine].reshape(384, 512), heads, 1, 1).reshape(4, 96, BLK)
        df[mine, part] = sums
        zs[mine, part] = sums.astype(BF)

    def project(half):
        cols = pl.ds(pl.multiple_of(half * FEAT, BLK), FEAT)
        return mm(attn[0], w_ref[:384, cols], 1, 0) + mm(attn[1], w_ref[384:, cols], 1, 0)

    attended_part(0)
    gsend.wait_recv()
    other_cols = pl.ds(pl.multiple_of((1 - hd) * FEAT, BLK), FEAT)
    for t in range(3):
        rows = slice(t * QB, (t + 1) * QB)
        part = (dpart[rows, :] + mm(w_ref[rows, other_cols], gfull[:, other_cols], 1, 1)).astype(BF)
        for n in range(4):
            dat[4 * t + n] = part[n * HD:(n + 1) * HD]
    d_remote, d_local = scatter_plan(dat, rd, s_d, r_da, r_dc)
    for copy in d_remote + d_local:
        copy.start()
    attended_part(1)
    attended_part(2)
    transposed_half(1 - hd)
    gy_far = gy_plan(1 - hd, 1)
    for copy in gy_far:
        copy.start()
    gy_far_fwd = gy_forward(hd, 0)
    forward_shared(dat, rd, s_df, r_dc)
    gy_arrived(hd, 0)
    for part in range(3):
        ay_arrived(part)
        weight_part(part, hd)
    z_first(hd)
    attended_rows()
    psend[...] = project(1 - hd).astype(BF)
    p_copy = rcopy(psend, precv, s_p.at[0], r_p.at[0], me, 1 - hd)
    p_copy.start()
    gy_far_fwd += gy_forward(1 - hd, 1)
    wait_shared(dat, rd, r_dc)
    lax.fori_loop(0, 1, bwd_item, 0)
    gy_arrived(1 - hd, 1)
    for part in range(3):
        weight_part(part, 1 - hd)
    z_first(1 - hd)
    lax.fori_loop(1, 3, bwd_item, 0)
    finish()
    z_second()
    pown[...] = project(hd)
    p_copy.wait_recv()
    proj_ref[...] = (pown[...] + precv[...].astype(F32)).astype(BF)
    stores = [lcopy(proj_ref, proj_hbm, s_out.at[3])]
    stores[0].start()

    for jj in range(4):
        for cc in range(2):
            lcopy(rout.at[0], rout.at[3 * jj + cc], r_o.at[3 * jj + cc]).wait()
        lcopy(rout.at[0, 0], rout.at[3 * jj + 2, 0], r_oq.at[3 * jj + 2]).wait()
        lcopy(rout.at[0, 1:3], rout.at[3 * jj + 2, 1:3], r_o.at[3 * jj + 2]).wait()
    for i, (ref, dst) in enumerate(((dq_ref, dq_hbm), (dk_ref, dk_hbm), (dv_ref, dv_hbm))):
        for t in range(6):
            tile = rout[2 * t:2 * t + 2, i].reshape(BLK, BLK)
            ref[:, t * BLK:(t + 1) * BLK] = tile.T
        stores.append(lcopy(ref, dst, s_out.at[i]))
        stores[-1].start()
    f_remote = []
    summed = df[z]
    for slot in range(3, 7):
        z_arrived(slot)
        summed = summed + rz[slot].astype(F32)
    for t in range(8):
        fin[t, :, :12, :] = summed[:, 12 * t:12 * t + 12]
    for m in range(1, 8):
        t = (s + m) % 8
        f_remote.append(rcopy(fin.at[t], rf.at[s], s_f.at[m], r_f.at[s], clip8 + t))
        f_remote[-1].start()
    rf[s] = fin[s]
    for m in range(1, 8):
        t = (s + m) % 8
        lcopy(rf.at[t], rf.at[t], r_f.at[t]).wait()
    for core in range(2):
        every = rf[core] + rf[2 + core] + rf[4 + core] + rf[6 + core]
        for part in range(3):
            lo = core * 384 + part * BLK
            dw_ref[:, lo:lo + BLK] = every[part, :12].astype(BF)
    for copy in stores:
        copy.wait()

    gsend.wait_send()
    for copy in d_remote + shared_plan(rx, s_xf, r_xc) + shared_plan(rd, s_df, r_dc) + gy_near[:2] + gy_far[:2] + gy_far_fwd + ay_remote + f_remote:
        copy.wait_send()
    xc_copy.wait_send()
    p_copy.wait_send()
    for n in range(4):
        at_send(0, n, "wait")

        @pl.when((c == 0) == (n in (0, 3)))
        def _(n=n):
            at_send(1, n, "wait")

    oq("wait")
    for b in range(8):
        own_send(b, "wait")
    okv("wait")
    for owner, to, slot in first_hops:
        z_copy(owner, to, slot).wait_send()
    for owner, to, slot, _ in second_hops:
        z_copy(owner, to, slot).wait_send()


def place(*refs):
    for i in range(5):
        refs[5 + i][...] = refs[i][...]


def local(queries, keys, values, w_out, grad_proj, frame_levels):
    vmem = pl.BlockSpec(memory_space=pltpu.VMEM)
    smem = pl.BlockSpec(memory_space=pltpu.SMEM)
    hbm = pl.BlockSpec(memory_space=pl.ANY)
    rows = jax.ShapeDtypeStruct((BLK, FEAT), BF)
    dma = lambda n: pltpu.SemaphoreType.DMA(n if isinstance(n, tuple) else (n,))
    scratch = [pltpu.VMEM((BLK, FEAT), BF)] * 4 + [dma(4)] + [pltpu.VMEM((BLK, FEAT), BF)] * 3 + [
        pltpu.VMEM((FEAT, WIDTH), BF),
        pltpu.VMEM((BLK, FEAT), BF),
        dma(5),
        pltpu.VMEM((12, 3, HD, BLK), BF),
        pltpu.VMEM((2, 3, HD, SLOTS), BF),
        pltpu.VMEM((12, HD, BLK), BF),
        pltpu.VMEM((2, HD, SLOTS), BF),
        pltpu.VMEM((BLK, WIDTH), BF),
        pltpu.VMEM((8, 4, 48, BLK), BF),
        pltpu.VMEM((8, 2, 48, 512), BF),
        pltpu.VMEM((2, 2, SLOTS, HD), BF),
        pltpu.VMEM((1, SLOTS), jnp.int32),
        pltpu.VMEM((2, 1, SLOTS), F32),
        pltpu.VMEM((2, 4, SLOTS, QB), F32),
        pltpu.VMEM((2, 4, SLOTS, QB), BF),
        pltpu.VMEM((2, SLOTS, QB), BF),
        pltpu.VMEM((2, HD, SLOTS), BF),
        pltpu.VMEM((12, HD, BLK), BF),
        pltpu.VMEM((2, BLK, 384), BF),
        pltpu.VMEM((BLK, FEAT), F32),
        pltpu.VMEM((BLK, FEAT), BF),
        pltpu.VMEM((BLK, FEAT), BF),
        pltpu.VMEM((2, 2, HD, SLOTS), F32),
        pltpu.VMEM((2, HD, 512), F32),
        pltpu.VMEM((2, 3, HD, SLOTS), BF),
        pltpu.VMEM((2, HD, 512), BF),
        pltpu.VMEM((12, 3, HD, BLK), BF),
        pltpu.VMEM((FEAT, BLK), F32),
        pltpu.VMEM((3, 2, HD, 512), BF),
        pltpu.VMEM((8, 3, 96, BLK), F32),
        pltpu.VMEM((8, 3, 96, BLK), BF),
        pltpu.VMEM((7, 3, 96, BLK), BF),
        pltpu.VMEM((8, 3, 16, BLK), F32),
        pltpu.VMEM((8, 3, 16, BLK), F32),
    ] + [
        dma(n)
        for n in (
            11, 3, 8, 8, 11, 3, 8, 8, 1, 1, (2, 3), (2, 4),
            (2, 8), 12, (3, 3), (3, 4), 1, 1, 1, 1, 8, 4, 4, 12, 12,
            7, 7, 8, 8,
        )
    ]
    proj, dq, dk, dv, dw = pl.pallas_call(
        kernel,
        out_shape=(rows, rows, rows, rows, jax.ShapeDtypeStruct((12, FEAT), BF)),
        in_specs=[hbm] * 5 + [smem],
        out_specs=[pl.BlockSpec(memory_space=pltpu.HBM)] * 4 + [vmem],
        scratch_shapes=scratch,
        compiler_params=pltpu.CompilerParams(
            collective_id=0, has_side_effects=True, vmem_limit_bytes=56 * 1024 * 1024
        ),
    )(queries, keys, values, w_out, grad_proj, frame_levels)
    strict = pl.BlockSpec(memory_space=pltpu.HBM)
    proj, dq, dk, dv, dw = pl.pallas_call(
        place,
        out_shape=(rows,) * 4 + (jax.ShapeDtypeStruct((12, FEAT), BF),),
        in_specs=[vmem] * 5,
        out_specs=[vmem] * 5,
        scratch_shapes=[],
    )(proj, dq, dk, dv, dw)
    return proj, dq, dk, dv, dw.T


def solution(mesh):
    rows = P("frame", "head")
    return jax.shard_map(
        local,
        mesh=mesh,
        in_specs=(rows, rows, rows, P("head", None), rows, P()),
        out_specs=(rows, rows, rows, rows, P("head", "frame")),
        check_vma=False,
    )
```

```python
import functools
import math

import jax
import jax.numpy as jnp
from jax import lax
from jax.experimental import pallas as pl
from jax.experimental.pallas import tpu as pltpu
from jax.sharding import PartitionSpec as P

MESH = pl.DeviceIdType.MESH
BF = jnp.bfloat16
F32 = jnp.float32
HD = 64
BLK = 128
QB = 256
SLOTS = 1024
FEAT = 768
WIDTH = 1536
FRAMES_CLIP = 16
EXP_SCALE = HD ** (-0.5) * math.log2(math.e)


def mm(left, right, dl, dr):
    return lax.dot_general(left, right, (((dl,), (dr,)), ((), ())), preferred_element_type=F32)


def lanes(block):
    return pl.ds(pl.multiple_of(block * BLK, BLK), BLK)


def kernel(
    q_hbm, k_hbm, v_hbm, w_hbm, g_hbm, lev_ref,
    proj_hbm, dq_hbm, dk_hbm, dv_hbm, dw_ref,
    proj_ref, dq_ref, dk_ref, dv_ref, s_out, q_ref, k_ref, v_ref, w_ref, g_ref, s_in, xt, rx, dat, rd, gfull, gt, gy, nat, lim_ref, inv_ref, prob, low, dsb,
    ot, att, attn, pown, psend, precv, acc, xc, dqkv, dkvc, rout,
    dpart, ayt, df, zs, rz, fin, rf,
    s_x, s_xf, r_xa, r_xc, s_d, s_df, r_da, r_dc, s_g, r_g, s_gy, r_gy,
    s_at, r_at, s_ay, r_ay, s_p, r_p, s_xc, r_xc2, s_o, s_oq, s_okv, r_o, r_oq,
    s_z, r_z, s_f, r_f,
):
    me = lax.axis_index("frame")
    hd = lax.axis_index("head")
    c = me % 2
    xl = (me // 2) % 2
    y = (me // 4) % 4
    z = me // 16
    s = me % 8
    clip8 = me - s
    j = s // 2
    sib = me + 1 - 2 * c
    far_y = 3 - y
    group = y // 2
    pos = group * 2 + c
    others = (3 - j, j + 1 - 2 * (j % 2), (j + 2) % 4)

    def rcopy(src, dst, ss, rs, dev, head=hd):
        return pltpu.make_async_remote_copy(
            src_ref=src, dst_ref=dst, send_sem=ss, recv_sem=rs,
            device_id=(dev, head), device_id_type=MESH,
        )

    def lcopy(src, dst, sem):
        return pltpu.make_async_copy(src, dst, sem)

    def ydev(core):
        return z * 16 + far_y * 4 + xl * 2 + core

    def zdev(zz):
        return zz * 16 + me % 16

    loads = [
        lcopy(src, dst, s_in.at[i])
        for i, (src, dst) in enumerate(
            ((q_hbm, q_ref), (k_hbm, k_ref), (v_hbm, v_ref), (g_hbm, g_ref), (w_hbm, w_ref))
        )
    ]
    for copy in loads:
        copy.start()

    bar = pltpu.get_barrier_semaphore()
    for d in range(1, 8):
        pl.semaphore_signal(bar, inc=1, device_id=(clip8 + (s + d) % 8, hd), device_id_type=MESH)
    pl.semaphore_signal(bar, inc=1, device_id=(me, 1 - hd), device_id_type=MESH)
    for core in range(2):
        pl.semaphore_signal(bar, inc=1, device_id=(ydev(core), hd), device_id_type=MESH)
    for d in (1, 2, 6, 7):
        pl.semaphore_signal(bar, inc=1, device_id=(zdev((z + d) % 8), hd), device_id_type=MESH)

    for i, ref in enumerate((q_ref, k_ref, v_ref)):
        loads[i].wait()
        for t in range(6):
            tile = ref[:, t * BLK:(t + 1) * BLK].T
            xt[2 * t, i] = tile[:HD]
            xt[2 * t + 1, i] = tile[HD:]
    pl.semaphore_wait(bar, 14)

    def scatter_plan(src, dst, ss, ra, rc):
        remote = []
        shared = []
        for n, jj in enumerate(others):
            base = clip8 + jj * 2
            remote.append(rcopy(src.at[3 * jj], dst.at[0, ..., lanes(s)], ss.at[3 * n], ra.at[s], base))
            remote.append(rcopy(src.at[3 * jj + 1], dst.at[0, ..., lanes(s)], ss.at[3 * n + 1], ra.at[s], base + 1))
            shared.append(rcopy(src.at[3 * jj + 2], dst.at[1, ..., lanes(s)], ss.at[3 * n + 2], rc.at[s], base + c))
        remote.append(rcopy(src.at[3 * j + 1 - c], dst.at[0, ..., lanes(s)], ss.at[9], ra.at[s], sib))
        shared.append(rcopy(src.at[3 * j + 2], dst.at[1, ..., lanes(s)], ss.at[10], rc.at[s], sib))
        local = [
            lcopy(src.at[3 * j + c], dst.at[0, ..., lanes(s)], ra.at[s]),
            lcopy(src.at[3 * j + 2], dst.at[1, ..., lanes(s)], rc.at[s]),
        ]
        return remote + shared, local

    def wait_own(src, dst, ra, rc):
        for b in range(8):
            lcopy(src.at[0], dst.at[0, ..., lanes(b)], ra.at[b]).wait()

    def shared_plan(dst, fs, rc):
        return [
            rcopy(dst.at[1, ..., lanes(jj * 2 + c)], dst.at[1, ..., lanes(jj * 2 + c)], fs.at[n], rc.at[jj * 2 + c], sib)
            for n, jj in enumerate(others)
        ]

    def forward_shared(src, dst, fs, rc):
        for copy, jj in zip(shared_plan(dst, fs, rc), others):
            lcopy(src.at[0], dst.at[1, ..., lanes(jj * 2 + c)], rc.at[jj * 2 + c]).wait()
            copy.start()
        lcopy(src.at[0], dst.at[1, ..., lanes(s)], rc.at[s]).wait()

    def wait_shared(src, dst, rc):
        for jj in range(4):
            b = jj * 2 + 1 - c
            lcopy(src.at[0], dst.at[1, ..., lanes(b)], rc.at[b]).wait()

    x_remote, x_local = scatter_plan(xt, rx, s_x, r_xa, r_xc)
    for copy in x_remote + x_local:
        copy.start()

    slot_iota = lax.broadcasted_iota(jnp.int32, (1, SLOTS), 1)
    seen = jnp.zeros((1, SLOTS), jnp.int32)
    start = jnp.int32(0)
    for f in range(FRAMES_CLIP):
        level = lev_ref[(me // 8) * FRAMES_CLIP + f]
        end = start + jnp.where(level == 0, BLK, jnp.where(level == 1, BLK // 4, BLK // 16))
        seen = jnp.where((slot_iota >= start) & (slot_iota < end), end, seen)
        start = end
    lim_ref[...] = seen

    def transposed_half(half):
        for t in range(6):
            cols = pl.ds(pl.multiple_of(half * FEAT + t * BLK, BLK), BLK)
            tile = gfull[:, cols].T
            for n in range(8):
                row = t * BLK + n * 16
                gt[4 * half + row // 192, (row % 192) // 48, row % 48:row % 48 + 16, :] = tile[n * 16:(n + 1) * 16]

    def gt_part(half, which_group):
        return gt.at[pl.ds(4 * half, 4), pl.ds(2 * which_group, 2)]

    def gy_part(half, p):
        return gy.at[pl.ds(4 * half, 4), :, :, lanes(p)]

    def gy_plan(half, which):
        return [
            rcopy(gt_part(half, 1 - group), gy_part(half, pos), s_gy.at[which, 0], r_gy.at[which, pos], ydev(c)),
            rcopy(gt_part(half, group), gy_part(half, pos), s_gy.at[which, 1], r_gy.at[which, pos], sib),
            lcopy(gt_part(half, group), gy_part(half, pos), r_gy.at[which, pos]),
        ]

    def gy_wait(half, which, p):
        lcopy(gt_part(half, group), gy_part(half, p), r_gy.at[which, p]).wait()

    def gy_forward(half, which):
        p = (1 - group) * 2 + c
        gy_wait(half, which, p)
        copy = rcopy(gy_part(half, p), gy_part(half, p), s_gy.at[which, 2], r_gy.at[which, p], sib)
        copy.start()
        return [copy]

    loads[3].wait()
    own_cols = pl.ds(pl.multiple_of(hd * FEAT, BLK), FEAT)
    gfull[:, own_cols] = g_ref[...]
    transposed_half(hd)
    loads[4].wait()
    for t in range(3):
        dpart[t * QB:(t + 1) * QB, :] = mm(w_ref[t * QB:(t + 1) * QB, own_cols], g_ref[...], 1, 1)
    for copy in x_remote[:7]:
        copy.wait_send()
    gsend = rcopy(g_ref, gfull.at[:, own_cols], s_g.at[0], r_g.at[0], me, 1 - hd)
    gsend.start()
    gy_near = gy_plan(hd, 0)
    for copy in gy_near:
        copy.start()
    wait_own(xt, rx, r_xa, r_xc)

    def naturals(slot):
        for i in range(2):
            nat[slot, i] = rx[slot, 1 + i].T

    naturals(0)

    def forward(ns, slot):
        q0s = [n * QB for n in ns]
        nks = [min(2 * n + 3, 8) for n in ns]
        qts = [rx[slot, 0, :, q0:q0 + QB] for q0 in q0s]
        lims = [lim_ref[:, q0:q0 + QB] for q0 in q0s]
        peaks = [jnp.full((8, QB), -1e30, F32) for _ in ns]
        work = [(kc, p) for kc in range(8) for p in range(2) if kc < nks[p]]
        for kc, p in work:
            rows = slice(kc * BLK, (kc + 1) * BLK)
            sc = mm(nat[slot, 0, rows, :], qts[p], 1, 0)
            if kc * BLK >= q0s[p]:
                key = lax.broadcasted_iota(jnp.int32, (BLK, QB), 0) + kc * BLK
                sc = jnp.where(key < lims[p], sc, -1e30)
            prob[slot, ns[p], rows, :] = sc
            peaks[p] = jnp.maximum(peaks[p], jnp.max(sc.reshape(BLK // 8, 8, QB), axis=0))
        peaks = [jnp.max(peak, axis=0, keepdims=True) for peak in peaks]
        totals = [jnp.zeros((8, QB), F32) for _ in ns]
        for kc, p in work:
            rows = slice(kc * BLK, (kc + 1) * BLK)
            ex = jnp.exp2((prob[slot, ns[p], rows, :] - peaks[p]) * EXP_SCALE)
            prob[slot, ns[p], rows, :] = ex
            totals[p] = totals[p] + jnp.sum(ex.reshape(BLK // 8, 8, QB), axis=0)
        totals = [jnp.sum(total, axis=0, keepdims=True) for total in totals]
        invs = [jnp.where(lim > 0, 1.0 / total, 0.0) for lim, total in zip(lims, totals)]
        for p in range(2):
            inv_ref[slot, :, q0s[p]:q0s[p] + QB] = invs[p]
        for kc, p in work:
            rows = slice(kc * BLK, (kc + 1) * BLK)
            low[slot, ns[p], rows, :] = (prob[slot, ns[p], rows, :] * invs[p]).astype(BF)
        for p in range(2):
            kl = nks[p] * BLK
            ot[slot, :, q0s[p]:q0s[p] + QB] = mm(rx[slot, 2, :, :kl], low[slot, ns[p], :kl, :], 1, 0).astype(BF)

    def backward(ns, slot):
        q0s = [n * QB for n in ns]
        nks = [min(2 * n + 3, 8) for n in ns]
        qts = [rx[slot, 0, :, q0:q0 + QB] for q0 in q0s]
        das = [rd[slot, :, q0:q0 + QB] for q0 in q0s]
        invs = [inv_ref[slot, :, q0:q0 + QB] for q0 in q0s]
        deltas = [
            jnp.sum(da.astype(F32) * ot[slot, :, q0:q0 + QB].astype(F32), axis=0, keepdims=True)
            for da, q0 in zip(das, q0s)
        ]
        for kc in range(8):
            rows = slice(kc * BLK, (kc + 1) * BLK)
            for p in range(2):
                if kc < nks[p]:
                    dp = mm(nat[slot, 1, rows, :], das[p], 1, 0)
                    dsb[p, rows, :] = (prob[slot, ns[p], rows, :] * invs[p] * (dp - deltas[p])).astype(BF)
        for p in range(2):
            kl = nks[p] * BLK
            dq = mm(rx[slot, 1, :, :kl], dsb[p, :kl, :], 1, 0) * HD ** (-0.5)
            dqkv[slot, 0, :, q0s[p]:q0s[p] + QB] = dq.astype(BF)
        for p in range(2):
            kl = nks[p] * BLK
            acc[slot, 0, :, :kl] += mm(qts[p], dsb[p, :kl, :], 1, 1)
            acc[slot, 1, :, :kl] += mm(das[p], low[slot, ns[p], :kl, :], 1, 1)

    def shared_send(src, dst, ss, rs, n, block, op):
        @pl.when(block == s)
        def _():
            if op == "start":
                lcopy(src, dst, rs).start()

        @pl.when(block != s)
        def _():
            copy = rcopy(src, dst, ss.at[n], rs, clip8 + block)
            copy.start() if op == "start" else copy.wait_send()

    def at_send(slot, n, op):
        head = 3 * j + c + slot * (2 - c)
        for b in (2 * n, 2 * n + 1):
            shared_send(ot.at[slot, :, lanes(b)], att.at[head], s_at.at[slot], r_at.at[head], b, b, op)

    def shared_block(n):
        return (1 - c) * (n + 4 * (n // 2)) + c * (n + 2)

    pairs = ((0, 3), (1, 2))

    def fwd_item(i, carry):
        slot = i // 2
        pair = jnp.where(i < 2, i, c)

        @pl.when(i == 1)
        def _():
            forward_shared(xt, rx, s_xf, r_xc)

        @pl.when(i == 2)
        def _():
            wait_shared(xt, rx, r_xc)
            naturals(1)

        for n in range(2):
            @pl.when(pair == n)
            def _(n=n):
                forward(pairs[n], slot)
                for qb in pairs[n]:
                    at_send(slot, qb, "start")

        return carry

    lax.fori_loop(0, 3, fwd_item, 0)

    acc[...] = jnp.zeros_like(acc)
    half_there = pl.ds(pl.multiple_of((1 - c) * 512, BLK), 512)
    half_here = pl.ds(pl.multiple_of(c * 512, BLK), 512)
    xc_copy = rcopy(acc.at[1, :, :, half_there], xc, s_xc.at[0], r_xc2.at[0], sib)

    def oq(op):
        for n in range(4):
            b = shared_block(n)
            shared_send(dqkv.at[1, 0, :, lanes(b)], rout.at[3 * j + 2, 0], s_oq, r_oq.at[3 * j + 2], n, b, op)

    def okv(op):
        for n in range(4):
            src = dkvc.at[:, :, n * BLK:(n + 1) * BLK]
            shared_send(src, rout.at[3 * j + 2, 1:3], s_okv, r_o.at[3 * j + 2], n, 4 * c + n, op)

    def own_send(b, op):
        shared_send(dqkv.at[0, :, :, lanes(b)], rout.at[3 * j + c], s_o, r_o.at[3 * j + c], b, b, op)

    def finish():
        dqkv[0, 1] = (acc[0, 0] * HD ** (-0.5)).astype(BF)
        dqkv[0, 2] = acc[0, 1].astype(BF)
        for b in range(8):
            own_send(b, "start")

    def bwd_item(i, carry):
        slot = jnp.where(i == 0, 1, 0)
        pair = jnp.where(i == 0, c, i - 1)

        @pl.when(i == 1)
        def _():
            xc_copy.start()
            oq("start")
            wait_own(dat, rd, r_da, r_dc)

        @pl.when(i == 2)
        def _():
            xc_copy.wait_recv()
            for part in range(2):
                scale = HD ** (-0.5) if part == 0 else 1.0
                dkvc[part] = ((acc[1, part, :, half_here] + xc[part]) * scale).astype(BF)
            okv("start")

        for n in range(2):
            @pl.when(pair == n)
            def _(n=n):
                backward(pairs[n], slot)

        return carry

    ay_remote = []

    def attended_part(part):
        for core in range(2):
            for h in range(2):
                lcopy(att.at[0], att.at[6 * core + 2 * part + h], r_at.at[6 * core + 2 * part + h]).wait()
        dst = ayt.at[part, :, :, lanes(pos)]
        for n, (core, dev) in enumerate(((0, ydev(0)), (1, ydev(1)), (1 - c, sib))):
            src = att.at[pl.ds(6 * core + 2 * part, 2)]
            ay_remote.append(rcopy(src, dst, s_ay.at[part, n], r_ay.at[part, pos], dev))
            ay_remote[-1].start()
        lcopy(att.at[pl.ds(6 * c + 2 * part, 2)], dst, r_ay.at[part, pos]).start()

    def attended_rows():
        for t in range(6):
            tile = att[2 * t:2 * t + 2].reshape(BLK, BLK).T
            attn[t // 3, :, (t % 3) * BLK:(t % 3 + 1) * BLK] = tile

    first_hops = ((4, 2, 0), (3, 1, 1), (5, 7, 2), (1, 1, 3), (7, 7, 4))
    second_hops = ((2, 2, 5, (0, 1)), (6, 6, 6, (2,)))

    def z_copy(owner, to, slot):
        return rcopy(zs.at[(z + owner) % 8], rz.at[slot], s_z.at[slot], r_z.at[slot], zdev((z + to) % 8))

    def z_arrived(slot):
        lcopy(rz.at[slot], rz.at[slot], r_z.at[slot]).wait()

    def z_first(half):
        for owner, to, slot in first_hops:
            @pl.when(((z + owner) % 8) // 4 == half)
            def _():
                z_copy(owner, to, slot).start()

    def z_second():
        for owner, to, slot, joined in second_hops:
            piece = df[(z + owner) % 8]
            for n in joined:
                z_arrived(n)
                piece = piece + rz[n].astype(F32)
            zs[(z + owner) % 8] = piece.astype(BF)
            z_copy(owner, to, slot).start()

    def gy_arrived(half, which):
        gy_wait(half, which, pos)
        for g in range(2):
            gy_wait(half, which, g * 2 + 1 - c)

    def ay_arrived(part):
        for p in range(4):
            dst = ayt.at[part, :, :, lanes(p)]
            lcopy(dst, dst, r_ay.at[part, p]).wait()

    def weight_part(part, half):
        mine = pl.ds(4 * half, 4)
        heads = ayt[part].reshape(BLK, 512)
        sums = mm(gy[mine].reshape(384, 512), heads, 1, 1).reshape(4, 96, BLK)
        df[mine, part] = sums
        zs[mine, part] = sums.astype(BF)

    def project(half):
        cols = pl.ds(pl.multiple_of(half * FEAT, BLK), FEAT)
        return mm(attn[0], w_ref[:384, cols], 1, 0) + mm(attn[1], w_ref[384:, cols], 1, 0)

    attended_part(0)
    gsend.wait_recv()
    other_cols = pl.ds(pl.multiple_of((1 - hd) * FEAT, BLK), FEAT)
    for t in range(3):
        rows = slice(t * QB, (t + 1) * QB)
        part = (dpart[rows, :] + mm(w_ref[rows, other_cols], gfull[:, other_cols], 1, 1)).astype(BF)
        for n in range(4):
            dat[4 * t + n] = part[n * HD:(n + 1) * HD]
    d_remote, d_local = scatter_plan(dat, rd, s_d, r_da, r_dc)
    for copy in d_remote + d_local:
        copy.start()
    attended_part(1)
    attended_part(2)
    transposed_half(1 - hd)
    gy_far = gy_plan(1 - hd, 1)
    for copy in gy_far:
        copy.start()
    gy_far_fwd = gy_forward(hd, 0)
    forward_shared(dat, rd, s_df, r_dc)
    gy_arrived(hd, 0)
    for part in range(3):
        ay_arrived(part)
        weight_part(part, hd)
    z_first(hd)
    attended_rows()
    psend[...] = project(1 - hd).astype(BF)
    p_copy = rcopy(psend, precv, s_p.at[0], r_p.at[0], me, 1 - hd)
    p_copy.start()
    gy_far_fwd += gy_forward(1 - hd, 1)
    wait_shared(dat, rd, r_dc)
    lax.fori_loop(0, 1, bwd_item, 0)
    gy_arrived(1 - hd, 1)
    for part in range(3):
        weight_part(part, 1 - hd)
    z_first(1 - hd)
    lax.fori_loop(1, 3, bwd_item, 0)
    finish()
    z_second()
    pown[...] = project(hd)
    p_copy.wait_recv()
    proj_ref[...] = (pown[...] + precv[...].astype(F32)).astype(BF)
    stores = [lcopy(proj_ref, proj_hbm, s_out.at[3])]
    stores[0].start()

    for jj in range(4):
        for cc in range(2):
            lcopy(rout.at[0], rout.at[3 * jj + cc], r_o.at[3 * jj + cc]).wait()
        lcopy(rout.at[0, 0], rout.at[3 * jj + 2, 0], r_oq.at[3 * jj + 2]).wait()
        lcopy(rout.at[0, 1:3], rout.at[3 * jj + 2, 1:3], r_o.at[3 * jj + 2]).wait()
    for i, (ref, dst) in enumerate(((dq_ref, dq_hbm), (dk_ref, dk_hbm), (dv_ref, dv_hbm))):
        for t in range(6):
            tile = rout[2 * t:2 * t + 2, i].reshape(BLK, BLK)
            ref[:, t * BLK:(t + 1) * BLK] = tile.T
        stores.append(lcopy(ref, dst, s_out.at[i]))
        stores[-1].start()
    f_remote = []
    summed = df[z]
    for slot in range(3, 7):
        z_arrived(slot)
        summed = summed + rz[slot].astype(F32)
    for t in range(8):
        fin[t, :, :12, :] = summed[:, 12 * t:12 * t + 12]
    for m in range(1, 8):
        t = (s + m) % 8
        f_remote.append(rcopy(fin.at[t], rf.at[s], s_f.at[m], r_f.at[s], clip8 + t))
        f_remote[-1].start()
    rf[s] = fin[s]
    for m in range(1, 8):
        t = (s + m) % 8
        lcopy(rf.at[t], rf.at[t], r_f.at[t]).wait()
    for core in range(2):
        every = rf[core] + rf[2 + core] + rf[4 + core] + rf[6 + core]
        for part in range(3):
            lo = core * 384 + part * BLK
            dw_ref[:, lo:lo + BLK] = every[part, :12].astype(BF)
    for copy in stores:
        copy.wait()

    gsend.wait_send()
    for copy in x_remote[7:] + d_remote + shared_plan(rx, s_xf, r_xc) + shared_plan(rd, s_df, r_dc) + gy_near[:2] + gy_far[:2] + gy_far_fwd + ay_remote + f_remote:
        copy.wait_send()
    xc_copy.wait_send()
    p_copy.wait_send()
    for n in range(4):
        at_send(0, n, "wait")

        @pl.when((c == 0) == (n in (0, 3)))
        def _(n=n):
            at_send(1, n, "wait")

    oq("wait")
    for b in range(8):
        own_send(b, "wait")
    okv("wait")
    for owner, to, slot in first_hops:
        z_copy(owner, to, slot).wait_send()
    for owner, to, slot, _ in second_hops:
        z_copy(owner, to, slot).wait_send()


def place(*refs):
    sems = refs[15]
    loads = [pltpu.make_async_copy(refs[i], refs[10 + i], sems.at[i]) for i in range(5)]
    stores = [pltpu.make_async_copy(refs[10 + i], refs[5 + i], sems.at[5 + i]) for i in range(5)]
    for copy in loads:
        copy.start()
    for load, store in zip(loads, stores):
        load.wait()
        store.start()
    for copy in stores:
        copy.wait()


def local(queries, keys, values, w_out, grad_proj, frame_levels):
    vmem = pl.BlockSpec(memory_space=pltpu.VMEM)
    smem = pl.BlockSpec(memory_space=pltpu.SMEM)
    hbm = pl.BlockSpec(memory_space=pl.ANY)
    rows = jax.ShapeDtypeStruct((BLK, FEAT), BF)
    dma = lambda n: pltpu.SemaphoreType.DMA(n if isinstance(n, tuple) else (n,))
    scratch = [pltpu.VMEM((BLK, FEAT), BF)] * 4 + [dma(4)] + [pltpu.VMEM((BLK, FEAT), BF)] * 3 + [
        pltpu.VMEM((FEAT, WIDTH), BF),
        pltpu.VMEM((BLK, FEAT), BF),
        dma(5),
        pltpu.VMEM((12, 3, HD, BLK), BF),
        pltpu.VMEM((2, 3, HD, SLOTS), BF),
        pltpu.VMEM((12, HD, BLK), BF),
        pltpu.VMEM((2, HD, SLOTS), BF),
        pltpu.VMEM((BLK, WIDTH), BF),
        pltpu.VMEM((8, 4, 48, BLK), BF),
        pltpu.VMEM((8, 2, 48, 512), BF),
        pltpu.VMEM((2, 2, SLOTS, HD), BF),
        pltpu.VMEM((1, SLOTS), jnp.int32),
        pltpu.VMEM((2, 1, SLOTS), F32),
        pltpu.VMEM((2, 4, SLOTS, QB), F32),
        pltpu.VMEM((2, 4, SLOTS, QB), BF),
        pltpu.VMEM((2, SLOTS, QB), BF),
        pltpu.VMEM((2, HD, SLOTS), BF),
        pltpu.VMEM((12, HD, BLK), BF),
        pltpu.VMEM((2, BLK, 384), BF),
        pltpu.VMEM((BLK, FEAT), F32),
        pltpu.VMEM((BLK, FEAT), BF),
        pltpu.VMEM((BLK, FEAT), BF),
        pltpu.VMEM((2, 2, HD, SLOTS), F32),
        pltpu.VMEM((2, HD, 512), F32),
        pltpu.VMEM((2, 3, HD, SLOTS), BF),
        pltpu.VMEM((2, HD, 512), BF),
        pltpu.VMEM((12, 3, HD, BLK), BF),
        pltpu.VMEM((FEAT, BLK), F32),
        pltpu.VMEM((3, 2, HD, 512), BF),
        pltpu.VMEM((8, 3, 96, BLK), F32),
        pltpu.VMEM((8, 3, 96, BLK), BF),
        pltpu.VMEM((7, 3, 96, BLK), BF),
        pltpu.VMEM((8, 3, 16, BLK), F32),
        pltpu.VMEM((8, 3, 16, BLK), F32),
    ] + [
        dma(n)
        for n in (
            11, 3, 8, 8, 11, 3, 8, 8, 1, 1, (2, 3), (2, 4),
            (2, 8), 12, (3, 3), (3, 4), 1, 1, 1, 1, 8, 4, 4, 12, 12,
            7, 7, 8, 8,
        )
    ]
    proj, dq, dk, dv, dw = pl.pallas_call(
        kernel,
        out_shape=(rows, rows, rows, rows, jax.ShapeDtypeStruct((12, FEAT), BF)),
        in_specs=[hbm] * 5 + [smem],
        out_specs=[pl.BlockSpec(memory_space=pltpu.HBM)] * 4 + [vmem],
        scratch_shapes=scratch,
        compiler_params=pltpu.CompilerParams(
            collective_id=0, has_side_effects=True, vmem_limit_bytes=56 * 1024 * 1024
        ),
    )(queries, keys, values, w_out, grad_proj, frame_levels)
    strict = pl.BlockSpec(memory_space=pltpu.HBM)
    proj, dq, dk, dv, dw = pl.pallas_call(
        place,
        out_shape=(rows,) * 4 + (jax.ShapeDtypeStruct((12, FEAT), BF),),
        in_specs=[strict] * 5,
        out_specs=[strict] * 5,
        scratch_shapes=[pltpu.VMEM((BLK, FEAT), BF)] * 4 + [pltpu.VMEM((12, FEAT), BF), dma(10)],
    )(proj, dq, dk, dv, dw)
    return proj, dq, dk, dv, dw.T


def solution(mesh):
    rows = P("frame", "head")
    return jax.shard_map(
        local,
        mesh=mesh,
        in_specs=(rows, rows, rows, P("head", None), rows, P()),
        out_specs=(rows, rows, rows, rows, P("head", "frame")),
        check_vma=False,
    )
```

```python
import functools
import math

import jax
import jax.numpy as jnp
from jax import lax
from jax.experimental import pallas as pl
from jax.experimental.pallas import tpu as pltpu
from jax.sharding import PartitionSpec as P

MESH = pl.DeviceIdType.MESH
BF = jnp.bfloat16
F32 = jnp.float32
HD = 64
BLK = 128
QB = 256
SLOTS = 1024
FEAT = 768
WIDTH = 1536
FRAMES_CLIP = 16
EXP_SCALE = HD ** (-0.5) * math.log2(math.e)


def mm(left, right, dl, dr):
    return lax.dot_general(left, right, (((dl,), (dr,)), ((), ())), preferred_element_type=F32)


def lanes(block):
    return pl.ds(pl.multiple_of(block * BLK, BLK), BLK)


def kernel(
    q_hbm, k_hbm, v_hbm, w_hbm, g_hbm, lev_ref,
    proj_hbm, dq_hbm, dk_hbm, dv_hbm, dw_ref,
    proj_ref, dq_ref, dk_ref, dv_ref, s_out, q_ref, k_ref, v_ref, w_ref, g_ref, s_in, xt, rx, dat, rd, gfull, gt, gy, nat, lim_ref, inv_ref, prob, low, dsb,
    ot, att, attn, pown, psend, precv, acc, xc, dqkv, dkvc, rout,
    dpart, ayt, df, zs, rz, fin, rf,
    s_x, s_xf, r_xa, r_xc, s_d, s_df, r_da, r_dc, s_g, r_g, s_gy, r_gy,
    s_at, r_at, s_ay, r_ay, s_p, r_p, s_xc, r_xc2, s_o, s_oq, s_okv, r_o, r_oq,
    s_z, r_z, s_f, r_f,
):
    me = lax.axis_index("frame")
    hd = lax.axis_index("head")
    c = me % 2
    xl = (me // 2) % 2
    y = (me // 4) % 4
    z = me // 16
    s = me % 8
    clip8 = me - s
    j = s // 2
    sib = me + 1 - 2 * c
    far_y = 3 - y
    group = y // 2
    pos = group * 2 + c
    others = (3 - j, j + 1 - 2 * (j % 2), (j + 2) % 4)

    def rcopy(src, dst, ss, rs, dev, head=hd):
        return pltpu.make_async_remote_copy(
            src_ref=src, dst_ref=dst, send_sem=ss, recv_sem=rs,
            device_id=(dev, head), device_id_type=MESH,
        )

    def lcopy(src, dst, sem):
        return pltpu.make_async_copy(src, dst, sem)

    def ydev(core):
        return z * 16 + far_y * 4 + xl * 2 + core

    def zdev(zz):
        return zz * 16 + me % 16

    loads = [
        lcopy(src, dst, s_in.at[i])
        for i, (src, dst) in enumerate(
            ((q_hbm, q_ref), (k_hbm, k_ref), (v_hbm, v_ref), (g_hbm, g_ref), (w_hbm, w_ref))
        )
    ]
    for copy in loads:
        copy.start()

    bar = pltpu.get_barrier_semaphore()
    for d in range(1, 8):
        pl.semaphore_signal(bar, inc=1, device_id=(clip8 + (s + d) % 8, hd), device_id_type=MESH)
    pl.semaphore_signal(bar, inc=1, device_id=(me, 1 - hd), device_id_type=MESH)
    for core in range(2):
        pl.semaphore_signal(bar, inc=1, device_id=(ydev(core), hd), device_id_type=MESH)
    for d in (1, 2, 6, 7):
        pl.semaphore_signal(bar, inc=1, device_id=(zdev((z + d) % 8), hd), device_id_type=MESH)

    for i, ref in enumerate((q_ref, k_ref, v_ref)):
        loads[i].wait()
        for t in range(6):
            tile = ref[:, t * BLK:(t + 1) * BLK].T
            xt[2 * t, i] = tile[:HD]
            xt[2 * t + 1, i] = tile[HD:]
    pl.semaphore_wait(bar, 14)

    def scatter_plan(src, dst, ss, ra, rc):
        remote = []
        shared = []
        for n, jj in enumerate(others):
            base = clip8 + jj * 2
            remote.append(rcopy(src.at[3 * jj], dst.at[0, ..., lanes(s)], ss.at[3 * n], ra.at[s], base))
            remote.append(rcopy(src.at[3 * jj + 1], dst.at[0, ..., lanes(s)], ss.at[3 * n + 1], ra.at[s], base + 1))
            shared.append(rcopy(src.at[3 * jj + 2], dst.at[1, ..., lanes(s)], ss.at[3 * n + 2], rc.at[s], base + c))
        remote.append(rcopy(src.at[3 * j + 1 - c], dst.at[0, ..., lanes(s)], ss.at[9], ra.at[s], sib))
        shared.append(rcopy(src.at[3 * j + 2], dst.at[1, ..., lanes(s)], ss.at[10], rc.at[s], sib))
        local = [
            lcopy(src.at[3 * j + c], dst.at[0, ..., lanes(s)], ra.at[s]),
            lcopy(src.at[3 * j + 2], dst.at[1, ..., lanes(s)], rc.at[s]),
        ]
        return remote + shared, local

    def wait_own(src, dst, ra, rc):
        for b in range(8):
            lcopy(src.at[0], dst.at[0, ..., lanes(b)], ra.at[b]).wait()

    def shared_plan(dst, fs, rc):
        return [
            rcopy(dst.at[1, ..., lanes(jj * 2 + c)], dst.at[1, ..., lanes(jj * 2 + c)], fs.at[n], rc.at[jj * 2 + c], sib)
            for n, jj in enumerate(others)
        ]

    def forward_shared(src, dst, fs, rc):
        for copy, jj in zip(shared_plan(dst, fs, rc), others):
            lcopy(src.at[0], dst.at[1, ..., lanes(jj * 2 + c)], rc.at[jj * 2 + c]).wait()
            copy.start()
        lcopy(src.at[0], dst.at[1, ..., lanes(s)], rc.at[s]).wait()

    def wait_shared(src, dst, rc):
        for jj in range(4):
            b = jj * 2 + 1 - c
            lcopy(src.at[0], dst.at[1, ..., lanes(b)], rc.at[b]).wait()

    x_remote, x_local = scatter_plan(xt, rx, s_x, r_xa, r_xc)
    for copy in x_remote + x_local:
        copy.start()

    slot_iota = lax.broadcasted_iota(jnp.int32, (1, SLOTS), 1)
    seen = jnp.zeros((1, SLOTS), jnp.int32)
    start = jnp.int32(0)
    for f in range(FRAMES_CLIP):
        level = lev_ref[(me // 8) * FRAMES_CLIP + f]
        end = start + jnp.where(level == 0, BLK, jnp.where(level == 1, BLK // 4, BLK // 16))
        seen = jnp.where((slot_iota >= start) & (slot_iota < end), end, seen)
        start = end
    lim_ref[...] = seen

    def transposed_half(half):
        for t in range(6):
            cols = pl.ds(pl.multiple_of(half * FEAT + t * BLK, BLK), BLK)
            tile = gfull[:, cols].T
            for n in range(8):
                row = t * BLK + n * 16
                gt[4 * half + row // 192, (row % 192) // 48, row % 48:row % 48 + 16, :] = tile[n * 16:(n + 1) * 16]

    def gt_part(half, which_group):
        return gt.at[pl.ds(4 * half, 4), pl.ds(2 * which_group, 2)]

    def gy_part(half, p):
        return gy.at[pl.ds(4 * half, 4), :, :, lanes(p)]

    def gy_plan(half, which):
        return [
            rcopy(gt_part(half, 1 - group), gy_part(half, pos), s_gy.at[which, 0], r_gy.at[which, pos], ydev(c)),
            rcopy(gt_part(half, group), gy_part(half, pos), s_gy.at[which, 1], r_gy.at[which, pos], sib),
            lcopy(gt_part(half, group), gy_part(half, pos), r_gy.at[which, pos]),
        ]

    def gy_wait(half, which, p):
        lcopy(gt_part(half, group), gy_part(half, p), r_gy.at[which, p]).wait()

    def gy_forward(half, which):
        p = (1 - group) * 2 + c
        gy_wait(half, which, p)
        copy = rcopy(gy_part(half, p), gy_part(half, p), s_gy.at[which, 2], r_gy.at[which, p], sib)
        copy.start()
        return [copy]

    loads[3].wait()
    own_cols = pl.ds(pl.multiple_of(hd * FEAT, BLK), FEAT)
    gfull[:, own_cols] = g_ref[...]
    transposed_half(hd)
    loads[4].wait()
    for t in range(3):
        dpart[t * QB:(t + 1) * QB, :] = mm(w_ref[t * QB:(t + 1) * QB, own_cols], g_ref[...], 1, 1)
    for copy in x_remote[:7]:
        copy.wait_send()
    gsend = rcopy(g_ref, gfull.at[:, own_cols], s_g.at[0], r_g.at[0], me, 1 - hd)
    gsend.start()
    gy_near = gy_plan(hd, 0)
    for copy in gy_near:
        copy.start()
    wait_own(xt, rx, r_xa, r_xc)

    def naturals(slot):
        for i in range(2):
            nat[slot, i] = rx[slot, 1 + i].T

    naturals(0)

    def forward(ns, slot):
        q0s = [n * QB for n in ns]
        nks = [min(2 * n + 3, 8) for n in ns]
        qts = [rx[slot, 0, :, q0:q0 + QB] for q0 in q0s]
        lims = [lim_ref[:, q0:q0 + QB] for q0 in q0s]
        peaks = [jnp.full((8, QB), -1e30, F32) for _ in ns]
        work = [(kc, p) for kc in range(8) for p in range(2) if kc < nks[p]]
        for kc, p in work:
            rows = slice(kc * BLK, (kc + 1) * BLK)
            sc = mm(nat[slot, 0, rows, :], qts[p], 1, 0)
            if kc * BLK >= q0s[p]:
                key = lax.broadcasted_iota(jnp.int32, (BLK, QB), 0) + kc * BLK
                sc = jnp.where(key < lims[p], sc, -1e30)
            prob[slot, ns[p], rows, :] = sc
            peaks[p] = jnp.maximum(peaks[p], jnp.max(sc.reshape(BLK // 8, 8, QB), axis=0))
        peaks = [jnp.max(peak, axis=0, keepdims=True) for peak in peaks]
        totals = [jnp.zeros((8, QB), F32) for _ in ns]
        for kc, p in work:
            rows = slice(kc * BLK, (kc + 1) * BLK)
            ex = jnp.exp2((prob[slot, ns[p], rows, :] - peaks[p]) * EXP_SCALE)
            prob[slot, ns[p], rows, :] = ex
            totals[p] = totals[p] + jnp.sum(ex.reshape(BLK // 8, 8, QB), axis=0)
        totals = [jnp.sum(total, axis=0, keepdims=True) for total in totals]
        invs = [jnp.where(lim > 0, 1.0 / total, 0.0) for lim, total in zip(lims, totals)]
        for p in range(2):
            inv_ref[slot, :, q0s[p]:q0s[p] + QB] = invs[p]
        for kc, p in work:
            rows = slice(kc * BLK, (kc + 1) * BLK)
            low[slot, ns[p], rows, :] = (prob[slot, ns[p], rows, :] * invs[p]).astype(BF)
        for p in range(2):
            kl = nks[p] * BLK
            ot[slot, :, q0s[p]:q0s[p] + QB] = mm(rx[slot, 2, :, :kl], low[slot, ns[p], :kl, :], 1, 0).astype(BF)

    def backward(ns, slot):
        q0s = [n * QB for n in ns]
        nks = [min(2 * n + 3, 8) for n in ns]
        qts = [rx[slot, 0, :, q0:q0 + QB] for q0 in q0s]
        das = [rd[slot, :, q0:q0 + QB] for q0 in q0s]
        invs = [inv_ref[slot, :, q0:q0 + QB] for q0 in q0s]
        deltas = [
            jnp.sum(da.astype(F32) * ot[slot, :, q0:q0 + QB].astype(F32), axis=0, keepdims=True)
            for da, q0 in zip(das, q0s)
        ]
        for kc in range(8):
            rows = slice(kc * BLK, (kc + 1) * BLK)
            for p in range(2):
                if kc < nks[p]:
                    dp = mm(nat[slot, 1, rows, :], das[p], 1, 0)
                    dsb[p, rows, :] = (prob[slot, ns[p], rows, :] * invs[p] * (dp - deltas[p])).astype(BF)
        for p in range(2):
            kl = nks[p] * BLK
            dq = mm(rx[slot, 1, :, :kl], dsb[p, :kl, :], 1, 0) * HD ** (-0.5)
            dqkv[slot, 0, :, q0s[p]:q0s[p] + QB] = dq.astype(BF)
        for p in range(2):
            kl = nks[p] * BLK
            acc[slot, 0, :, :kl] += mm(qts[p], dsb[p, :kl, :], 1, 1)
            acc[slot, 1, :, :kl] += mm(das[p], low[slot, ns[p], :kl, :], 1, 1)

    def shared_send(src, dst, ss, rs, n, block, op):
        @pl.when(block == s)
        def _():
            if op == "start":
                lcopy(src, dst, rs).start()

        @pl.when(block != s)
        def _():
            copy = rcopy(src, dst, ss.at[n], rs, clip8 + block)
            copy.start() if op == "start" else copy.wait_send()

    def at_send(slot, n, op):
        head = 3 * j + c + slot * (2 - c)
        for b in (2 * n, 2 * n + 1):
            shared_send(ot.at[slot, :, lanes(b)], att.at[head], s_at.at[slot], r_at.at[head], b, b, op)

    def shared_block(n):
        return (1 - c) * (n + 4 * (n // 2)) + c * (n + 2)

    pairs = ((0, 3), (1, 2))

    def fwd_item(i, carry):
        slot = i // 2
        pair = jnp.where(i < 2, i, c)

        @pl.when(i == 1)
        def _():
            forward_shared(xt, rx, s_xf, r_xc)

        @pl.when(i == 2)
        def _():
            wait_shared(xt, rx, r_xc)
            naturals(1)

        for n in range(2):
            @pl.when(pair == n)
            def _(n=n):
                forward(pairs[n], slot)
                for qb in pairs[n]:
                    at_send(slot, qb, "start")

        return carry

    lax.fori_loop(0, 3, fwd_item, 0)

    acc[...] = jnp.zeros_like(acc)
    half_there = pl.ds(pl.multiple_of((1 - c) * 512, BLK), 512)
    half_here = pl.ds(pl.multiple_of(c * 512, BLK), 512)
    xc_copy = rcopy(acc.at[1, :, :, half_there], xc, s_xc.at[0], r_xc2.at[0], sib)

    def oq(op):
        for n in range(4):
            b = shared_block(n)
            shared_send(dqkv.at[1, 0, :, lanes(b)], rout.at[3 * j + 2, 0], s_oq, r_oq.at[3 * j + 2], n, b, op)

    def okv(op):
        for n in range(4):
            src = dkvc.at[:, :, n * BLK:(n + 1) * BLK]
            shared_send(src, rout.at[3 * j + 2, 1:3], s_okv, r_o.at[3 * j + 2], n, 4 * c + n, op)

    def own_send(b, op):
        shared_send(dqkv.at[0, :, :, lanes(b)], rout.at[3 * j + c], s_o, r_o.at[3 * j + c], b, b, op)

    def finish():
        dqkv[0, 1] = (acc[0, 0] * HD ** (-0.5)).astype(BF)
        dqkv[0, 2] = acc[0, 1].astype(BF)
        for b in range(8):
            own_send(b, "start")

    def bwd_item(i, carry):
        slot = jnp.where(i == 0, 1, 0)
        pair = jnp.where(i == 0, c, i - 1)

        @pl.when(i == 1)
        def _():
            xc_copy.start()
            oq("start")
            wait_own(dat, rd, r_da, r_dc)

        @pl.when(i == 2)
        def _():
            xc_copy.wait_recv()
            for part in range(2):
                scale = HD ** (-0.5) if part == 0 else 1.0
                dkvc[part] = ((acc[1, part, :, half_here] + xc[part]) * scale).astype(BF)
            okv("start")

        for n in range(2):
            @pl.when(pair == n)
            def _(n=n):
                backward(pairs[n], slot)

        return carry

    ay_remote = []

    def attended_part(part):
        for core in range(2):
            for h in range(2):
                lcopy(att.at[0], att.at[6 * core + 2 * part + h], r_at.at[6 * core + 2 * part + h]).wait()
        dst = ayt.at[part, :, :, lanes(pos)]
        for n, (core, dev) in enumerate(((0, ydev(0)), (1, ydev(1)), (1 - c, sib))):
            src = att.at[pl.ds(6 * core + 2 * part, 2)]
            ay_remote.append(rcopy(src, dst, s_ay.at[part, n], r_ay.at[part, pos], dev))
            ay_remote[-1].start()
        lcopy(att.at[pl.ds(6 * c + 2 * part, 2)], dst, r_ay.at[part, pos]).start()

    def attended_rows():
        for t in range(6):
            tile = att[2 * t:2 * t + 2].reshape(BLK, BLK).T
            attn[t // 3, :, (t % 3) * BLK:(t % 3 + 1) * BLK] = tile

    first_hops = ((4, 2, 0), (3, 1, 1), (5, 7, 2), (1, 1, 3), (7, 7, 4))
    second_hops = ((2, 2, 5, (0, 1)), (6, 6, 6, (2,)))

    def z_copy(owner, to, slot):
        return rcopy(zs.at[(z + owner) % 8], rz.at[slot], s_z.at[slot], r_z.at[slot], zdev((z + to) % 8))

    def z_arrived(slot):
        lcopy(rz.at[slot], rz.at[slot], r_z.at[slot]).wait()

    def z_first(half):
        for owner, to, slot in first_hops:
            @pl.when(((z + owner) % 8) // 4 == half)
            def _():
                z_copy(owner, to, slot).start()

    def z_second():
        for owner, to, slot, joined in second_hops:
            piece = df[(z + owner) % 8]
            for n in joined:
                z_arrived(n)
                piece = piece + rz[n].astype(F32)
            zs[(z + owner) % 8] = piece.astype(BF)
            z_copy(owner, to, slot).start()

    def gy_arrived(half, which):
        gy_wait(half, which, pos)
        for g in range(2):
            gy_wait(half, which, g * 2 + 1 - c)

    def ay_arrived(part):
        for p in range(4):
            dst = ayt.at[part, :, :, lanes(p)]
            lcopy(dst, dst, r_ay.at[part, p]).wait()

    def weight_part(part, half):
        mine = pl.ds(4 * half, 4)
        heads = ayt[part].reshape(BLK, 512)
        sums = mm(gy[mine].reshape(384, 512), heads, 1, 1).reshape(4, 96, BLK)
        df[mine, part] = sums
        zs[mine, part] = sums.astype(BF)

    def project(half):
        cols = pl.ds(pl.multiple_of(half * FEAT, BLK), FEAT)
        return mm(attn[0], w_ref[:384, cols], 1, 0) + mm(attn[1], w_ref[384:, cols], 1, 0)

    attended_part(0)
    gsend.wait_recv()
    transposed_half(1 - hd)
    gy_far = gy_plan(1 - hd, 1)
    for copy in gy_far:
        copy.start()
    other_cols = pl.ds(pl.multiple_of((1 - hd) * FEAT, BLK), FEAT)
    for t in range(3):
        rows = slice(t * QB, (t + 1) * QB)
        part = (dpart[rows, :] + mm(w_ref[rows, other_cols], gfull[:, other_cols], 1, 1)).astype(BF)
        for n in range(4):
            dat[4 * t + n] = part[n * HD:(n + 1) * HD]
    d_remote, d_local = scatter_plan(dat, rd, s_d, r_da, r_dc)
    for copy in d_remote + d_local:
        copy.start()
    attended_part(1)
    attended_part(2)
    gy_far_fwd = gy_forward(hd, 0)
    forward_shared(dat, rd, s_df, r_dc)
    gy_arrived(hd, 0)
    for part in range(3):
        ay_arrived(part)
        weight_part(part, hd)
    z_first(hd)
    attended_rows()
    psend[...] = project(1 - hd).astype(BF)
    p_copy = rcopy(psend, precv, s_p.at[0], r_p.at[0], me, 1 - hd)
    p_copy.start()
    gy_far_fwd += gy_forward(1 - hd, 1)
    wait_shared(dat, rd, r_dc)
    lax.fori_loop(0, 1, bwd_item, 0)
    gy_arrived(1 - hd, 1)
    for part in range(3):
        weight_part(part, 1 - hd)
    z_first(1 - hd)
    lax.fori_loop(1, 3, bwd_item, 0)
    finish()
    z_second()
    pown[...] = project(hd)
    p_copy.wait_recv()
    proj_ref[...] = (pown[...] + precv[...].astype(F32)).astype(BF)
    stores = [lcopy(proj_ref, proj_hbm, s_out.at[3])]
    stores[0].start()

    for jj in range(4):
        for cc in range(2):
            lcopy(rout.at[0], rout.at[3 * jj + cc], r_o.at[3 * jj + cc]).wait()
        lcopy(rout.at[0, 0], rout.at[3 * jj + 2, 0], r_oq.at[3 * jj + 2]).wait()
        lcopy(rout.at[0, 1:3], rout.at[3 * jj + 2, 1:3], r_o.at[3 * jj + 2]).wait()
    for i, (ref, dst) in enumerate(((dq_ref, dq_hbm), (dk_ref, dk_hbm), (dv_ref, dv_hbm))):
        for t in range(6):
            tile = rout[2 * t:2 * t + 2, i].reshape(BLK, BLK)
            ref[:, t * BLK:(t + 1) * BLK] = tile.T
        stores.append(lcopy(ref, dst, s_out.at[i]))
        stores[-1].start()
    f_remote = []
    summed = df[z]
    for slot in range(3, 7):
        z_arrived(slot)
        summed = summed + rz[slot].astype(F32)
    for t in range(8):
        fin[t, :, :12, :] = summed[:, 12 * t:12 * t + 12]
    for m in range(1, 8):
        t = (s + m) % 8
        f_remote.append(rcopy(fin.at[t], rf.at[s], s_f.at[m], r_f.at[s], clip8 + t))
        f_remote[-1].start()
    rf[s] = fin[s]
    for m in range(1, 8):
        t = (s + m) % 8
        lcopy(rf.at[t], rf.at[t], r_f.at[t]).wait()
    for core in range(2):
        every = rf[core] + rf[2 + core] + rf[4 + core] + rf[6 + core]
        for part in range(3):
            lo = core * 384 + part * BLK
            dw_ref[:, lo:lo + BLK] = every[part, :12].astype(BF)
    for copy in stores:
        copy.wait()

    gsend.wait_send()
    for copy in x_remote[7:] + d_remote + shared_plan(rx, s_xf, r_xc) + shared_plan(rd, s_df, r_dc) + gy_near[:2] + gy_far[:2] + gy_far_fwd + ay_remote + f_remote:
        copy.wait_send()
    xc_copy.wait_send()
    p_copy.wait_send()
    for n in range(4):
        at_send(0, n, "wait")

        @pl.when((c == 0) == (n in (0, 3)))
        def _(n=n):
            at_send(1, n, "wait")

    oq("wait")
    for b in range(8):
        own_send(b, "wait")
    okv("wait")
    for owner, to, slot in first_hops:
        z_copy(owner, to, slot).wait_send()
    for owner, to, slot, _ in second_hops:
        z_copy(owner, to, slot).wait_send()


def place(*refs):
    sems = refs[15]
    loads = [pltpu.make_async_copy(refs[i], refs[10 + i], sems.at[i]) for i in range(5)]
    stores = [pltpu.make_async_copy(refs[10 + i], refs[5 + i], sems.at[5 + i]) for i in range(5)]
    for copy in loads:
        copy.start()
    for load, store in zip(loads, stores):
        load.wait()
        store.start()
    for copy in stores:
        copy.wait()


def local(queries, keys, values, w_out, grad_proj, frame_levels):
    vmem = pl.BlockSpec(memory_space=pltpu.VMEM)
    smem = pl.BlockSpec(memory_space=pltpu.SMEM)
    hbm = pl.BlockSpec(memory_space=pl.ANY)
    rows = jax.ShapeDtypeStruct((BLK, FEAT), BF)
    dma = lambda n: pltpu.SemaphoreType.DMA(n if isinstance(n, tuple) else (n,))
    scratch = [pltpu.VMEM((BLK, FEAT), BF)] * 4 + [dma(4)] + [pltpu.VMEM((BLK, FEAT), BF)] * 3 + [
        pltpu.VMEM((FEAT, WIDTH), BF),
        pltpu.VMEM((BLK, FEAT), BF),
        dma(5),
        pltpu.VMEM((12, 3, HD, BLK), BF),
        pltpu.VMEM((2, 3, HD, SLOTS), BF),
        pltpu.VMEM((12, HD, BLK), BF),
        pltpu.VMEM((2, HD, SLOTS), BF),
        pltpu.VMEM((BLK, WIDTH), BF),
        pltpu.VMEM((8, 4, 48, BLK), BF),
        pltpu.VMEM((8, 2, 48, 512), BF),
        pltpu.VMEM((2, 2, SLOTS, HD), BF),
        pltpu.VMEM((1, SLOTS), jnp.int32),
        pltpu.VMEM((2, 1, SLOTS), F32),
        pltpu.VMEM((2, 4, SLOTS, QB), F32),
        pltpu.VMEM((2, 4, SLOTS, QB), BF),
        pltpu.VMEM((2, SLOTS, QB), BF),
        pltpu.VMEM((2, HD, SLOTS), BF),
        pltpu.VMEM((12, HD, BLK), BF),
        pltpu.VMEM((2, BLK, 384), BF),
        pltpu.VMEM((BLK, FEAT), F32),
        pltpu.VMEM((BLK, FEAT), BF),
        pltpu.VMEM((BLK, FEAT), BF),
        pltpu.VMEM((2, 2, HD, SLOTS), F32),
        pltpu.VMEM((2, HD, 512), F32),
        pltpu.VMEM((2, 3, HD, SLOTS), BF),
        pltpu.VMEM((2, HD, 512), BF),
        pltpu.VMEM((12, 3, HD, BLK), BF),
        pltpu.VMEM((FEAT, BLK), F32),
        pltpu.VMEM((3, 2, HD, 512), BF),
        pltpu.VMEM((8, 3, 96, BLK), F32),
        pltpu.VMEM((8, 3, 96, BLK), BF),
        pltpu.VMEM((7, 3, 96, BLK), BF),
        pltpu.VMEM((8, 3, 16, BLK), F32),
        pltpu.VMEM((8, 3, 16, BLK), F32),
    ] + [
        dma(n)
        for n in (
            11, 3, 8, 8, 11, 3, 8, 8, 1, 1, (2, 3), (2, 4),
            (2, 8), 12, (3, 3), (3, 4), 1, 1, 1, 1, 8, 4, 4, 12, 12,
            7, 7, 8, 8,
        )
    ]
    proj, dq, dk, dv, dw = pl.pallas_call(
        kernel,
        out_shape=(rows, rows, rows, rows, jax.ShapeDtypeStruct((12, FEAT), BF)),
        in_specs=[hbm] * 5 + [smem],
        out_specs=[pl.BlockSpec(memory_space=pltpu.HBM)] * 4 + [vmem],
        scratch_shapes=scratch,
        compiler_params=pltpu.CompilerParams(
            collective_id=0, has_side_effects=True, vmem_limit_bytes=56 * 1024 * 1024
        ),
    )(queries, keys, values, w_out, grad_proj, frame_levels)
    strict = pl.BlockSpec(memory_space=pltpu.HBM)
    proj, dq, dk, dv, dw = pl.pallas_call(
        place,
        out_shape=(rows,) * 4 + (jax.ShapeDtypeStruct((12, FEAT), BF),),
        in_specs=[strict] * 5,
        out_specs=[strict] * 5,
        scratch_shapes=[pltpu.VMEM((BLK, FEAT), BF)] * 4 + [pltpu.VMEM((12, FEAT), BF), dma(10)],
    )(proj, dq, dk, dv, dw)
    return proj, dq, dk, dv, dw.T


def solution(mesh):
    rows = P("frame", "head")
    return jax.shard_map(
        local,
        mesh=mesh,
        in_specs=(rows, rows, rows, P("head", None), rows, P()),
        out_specs=(rows, rows, rows, rows, P("head", "frame")),
        check_vma=False,
    )
```
